512 devices in a mesh: seq: 64 (over z, x, core), mp: 8 (over y).
Axes of the slice: x: 4, y: 8, z: 8, core: 2. Of those that a mesh axis runs over, the one named last changes fastest.
Arguments:
- frames_tokens: bfloat16 [8192, 8192], P('seq', 'mp')
- positions: int32 [8192, 3], P('seq'), may hold values from 0 to 1471, as said below
- norm_gain: bfloat16 [8192], replicated, may hold values from 0.099609375 to 1.8984375
- w_query: bfloat16 [8192, 4096], P('seq', 'mp'), may hold values from -0.109375 to 0.109375
- w_key: bfloat16 [8192, 512], P('seq'), may hold values from -0.109375 to 0.109375
- w_value: bfloat16 [8192, 512], P('seq'), may hold values from -0.0625 to 0.0625
- b_query: bfloat16 [4096], P('mp')
- b_key: bfloat16 [512], replicated
- b_value: bfloat16 [512], replicated, may hold values from -3 to 3
Outputs:
- attended: bfloat16 [8192, 4096], P('seq', 'mp')
The draws below stay inside these ranges and needn't reach their ends.
Inputs may be any that keep to these rules, and one draw needn't show every extreme that they name: Row k of positions belongs to the token in row k of frames_tokens. Tokens come in clips of whole frames; a token's ids are its frame, grid row and grid column inside its clip plus the clip's start, and each clip starts beyond every id of the clips before it.
All inputs are finite; a program needn't handle non-finite values.
Results may differ from the reference program's by a relative error of at most 0.01.
The reference program's roundings to bfloat16 on the way count: a program that leaves them out, or rounds other values in their place, can miss the bound.
Values may be sent and summed in bfloat16 or wider, within the bound.
A program may use at most 64 MiB of HBM per device.

```python
import math
import jax
import jax.numpy as jnp
from jax import lax

D = 8192
HD = 128
HQ = 32
HK = 4
TOK_DEV = 128
BLK = 2
TOKENS = 8192


def draw_frames_tokens(key, part):
    key = jax.random.fold_in(key, 11)
    key_one, key_two, key_three = jax.random.split(key, 3)
    col_scale = jnp.exp(jax.random.uniform(key_three, (1, D), minval=0.0, maxval=math.log(10.0)))
    row_scale = jnp.exp(jax.random.uniform(key_two, (TOKENS, 1), minval=0.0, maxval=math.log(10.0)))
    base_vals = jax.random.normal(key_one, (TOKENS, D), dtype=jnp.float32)
    return (base_vals * row_scale * col_scale).astype(jnp.bfloat16)


def draw_positions(key, part):
    key = jax.random.fold_in(key, 5)
    row_ids = jnp.arange(TOKENS, dtype=jnp.int32)
    source = row_ids // TOK_DEV
    within = row_ids % TOK_DEV
    seq_place = within // BLK * TOK_DEV + source * BLK + within % BLK
    clip_tokens = 512
    frame_tokens = 256
    clip_count = TOKENS // clip_tokens
    width_table = jnp.array([8, 16, 32], dtype=jnp.int32)
    picks = jax.random.randint(key, (clip_count,), 0, 3)
    last_pick = 2 * (picks[clip_count - 1] % 2)
    picks = jnp.where(jnp.arange(clip_count) == clip_count - 1, last_pick, picks)
    widths = width_table[picks]
    starts = 96 * jnp.arange(clip_count, dtype=jnp.int32)
    clip_id = seq_place // clip_tokens
    inside = seq_place % clip_tokens
    frame_idx = inside // frame_tokens
    in_frame = inside % frame_tokens
    clip_width = widths[clip_id]
    row_idx = in_frame // clip_width
    col_idx = in_frame % clip_width
    clip_start = starts[clip_id]
    return jnp.stack([frame_idx + clip_start, row_idx + clip_start, col_idx + clip_start], axis=1).astype(jnp.int32)


def draw_b_key(key, part):
    key = jax.random.fold_in(key, 21)
    return jax.random.normal(key, (HK * HD,), dtype=jnp.float32).astype(jnp.bfloat16)


def draw_b_query(key, part):
    key = jax.random.fold_in(key, 37)
    return jax.random.normal(key, (HQ * HD,), dtype=jnp.float32).astype(jnp.bfloat16)


def levels(key, dims, cuts, low, top_value):
    def one(axis_at, blocks):
        heights = jax.random.uniform(jax.random.fold_in(jax.random.fold_in(key, 6), axis_at), (blocks,), jnp.float32, low / len(cuts), top_value / len(cuts))
        return jnp.repeat(jnp.exp(heights), dims[axis_at] // blocks).reshape((-1,) + (1,) * (len(dims) - axis_at - 1))

    gain = one(*cuts[0])
    for cut in cuts[1:]:
        gain = gain * one(*cut)
    return gain


def gaussian(rng, dims, deviation, reach, cuts=(), held_as=jnp.bfloat16):
    entries = deviation * jax.random.normal(rng, dims, jnp.float32)
    if cuts:
        entries = entries * levels(rng, dims, cuts, -0.22, 0.18)
    return jnp.clip(entries, -reach, reach).astype(held_as)


def setup_inputs(seed: int = 0) -> dict:
    keys = jax.random.split(jax.random.key(seed), 10)
    frames_tokens = draw_frames_tokens(jax.random.fold_in(keys[9], 71), 0)
    positions = draw_positions(jax.random.fold_in(keys[9], 71), 0)
    norm_gain = jnp.clip(1.0 + 0.18 * jax.random.normal(keys[2], (D,), jnp.float32), 0.099609375, 1.8984375).astype(jnp.bfloat16)
    w_query = gaussian(keys[3], (D, HQ * HD), (D // 3) ** -0.5, 0.109375, ((0, 64), (1, 8)))
    w_key = gaussian(keys[4], (D, HK * HD), (D // 3) ** -0.5, 0.109375, ((0, 64),))
    w_value = gaussian(keys[5], (D, HK * HD), D ** -0.5, 0.0625, ((0, 64),))
    b_query = draw_b_query(jax.random.fold_in(keys[9], 71), 0)
    b_key = draw_b_key(jax.random.fold_in(keys[9], 71), 0)
    b_value = gaussian(keys[8], (HK * HD,), 0.5, 3.0)
    return dict(frames_tokens=frames_tokens, positions=positions, norm_gain=norm_gain, w_query=w_query, w_key=w_key, w_value=w_value, b_query=b_query, b_key=b_key, b_value=b_value)


def rotary_angles(rope_ids, half_dim):
    freq_index = jnp.arange(half_dim)
    frequency = jnp.power(1000000.0, -(2.0 * freq_index.astype(jnp.float32)) / (2 * half_dim))
    section = jnp.where(freq_index < 2 * half_dim // 8, 0, jnp.where(freq_index < 5 * 2 * half_dim // 16, 1, 2))
    chosen = jnp.where(section[None, :] == 0, rope_ids[:, 0:1], jnp.where(section[None, :] == 1, rope_ids[:, 1:2], rope_ids[:, 2:3]))
    return chosen.astype(jnp.float32) * frequency[None, :].astype(jnp.float32)

def rotate(linear, angles, heads):
    row_count = linear.shape[0]
    half_dim = angles.shape[1]
    halves = linear.reshape(row_count, heads, 2, half_dim)
    cosine = jnp.cos(angles)[:, None, :]
    sines = jnp.sin(angles)[:, None, :]
    front_half = halves[:, :, 0, :]
    back_half = halves[:, :, 1, :]
    turned = jnp.stack([front_half * cosine - back_half * sines, back_half * cosine + front_half * sines], axis=2)
    return turned.reshape(row_count, heads * 2 * half_dim).astype(jnp.bfloat16)

def reference(frames_tokens, positions, norm_gain, w_query, w_key, w_value, b_query, b_key, b_value):
    seq_count = TOKENS // TOK_DEV
    tokens = frames_tokens.reshape(seq_count, seq_count, BLK, D).transpose(1, 0, 2, 3).reshape(TOKENS, D)
    rope_ids = positions.reshape(seq_count, seq_count, BLK, 3).transpose(1, 0, 2, 3).reshape(TOKENS, 3)
    widened = tokens.astype(jnp.float32)
    inverse = lax.rsqrt(lax.optimization_barrier(jnp.mean(widened * widened, axis=1, keepdims=True)) + 1e-06)
    normed = (widened * inverse * norm_gain.astype(jnp.float32)[None, :]).astype(jnp.bfloat16)
    query_linear = jnp.dot(normed, w_query, preferred_element_type=jnp.float32) + b_query.astype(jnp.float32)[None, :]
    key_linear = jnp.dot(normed, w_key, preferred_element_type=jnp.float32) + b_key.astype(jnp.float32)[None, :]
    value_rows = (jnp.dot(normed, w_value, preferred_element_type=jnp.float32) + b_value.astype(jnp.float32)[None, :]).astype(jnp.bfloat16)
    angles = rotary_angles(rope_ids, HD // 2)
    queries = rotate(query_linear, angles, HQ).reshape(TOKENS, HQ, HD).transpose(1, 0, 2)
    key_rot = rotate(key_linear, angles, HK).reshape(TOKENS, HK, HD).transpose(1, 0, 2)
    value_heads = value_rows.reshape(TOKENS, HK, HD).transpose(1, 0, 2)
    seq_order = jnp.arange(TOKENS, dtype=jnp.int32)
    visible = seq_order[None, :] <= seq_order[:, None]
    group_size = HQ // HK
    softscale = 1.0 / math.sqrt(HD)

    def one_head(head_index):
        q_head = queries[head_index]
        k_head = key_rot[head_index // group_size]
        v_head = value_heads[head_index // group_size]
        scores = jnp.dot(q_head, k_head.T, preferred_element_type=jnp.float32) * softscale
        masked = jnp.where(visible, scores, -1e+30)
        row_max = lax.optimization_barrier(jnp.max(masked, axis=1, keepdims=True))
        exp_terms = jnp.where(visible, jnp.exp(masked - row_max), 0.0)
        denominator = lax.optimization_barrier(jnp.sum(exp_terms, axis=1, keepdims=True))
        mixture = jnp.dot(exp_terms.astype(jnp.bfloat16), v_head, preferred_element_type=jnp.float32)
        return (mixture / denominator).astype(jnp.bfloat16)
    heads = lax.map(one_head, jnp.arange(HQ, dtype=jnp.int32))
    return heads.transpose(1, 0, 2).reshape(TOKENS, HQ * HD)
```

```python
import functools
import math

import jax
import jax.numpy as jnp
import numpy as np
from jax import lax
from jax.experimental import pallas as pl
from jax.experimental.pallas import tpu as pltpu
from jax.sharding import PartitionSpec as P

HD = 128
T = 128
NX, NZ, NM = 4, 8, 8
NS = NZ * NX * 2
CA, CB = 256, 384
MESH = pl.DeviceIdType.MESH
DIST = [[0], [-1, 1], [-2, 2], [-3, 3], [4]]
EXP_SCALE = math.log2(math.e) / math.sqrt(HD)


class Gather:
    def __init__(self, a, b, sems, z, x, c, m):
        self.a, self.b = a, b
        self.ra, self.rb, self.ca, self.cb, self.sza, self.sxa, self.szb, self.sxb, self.sca, self.scb = sems
        self.z, self.x, self.c, self.m = z, x, c, m
        self.dir = 1 - 2 * c
        self.sent = []

    def rows(self, ref, dz, dx, core):
        block = (((self.z + dz + NZ) % NZ) * NX + (self.x + dx) % NX) * 2 + core
        return ref.at[pl.ds(pl.multiple_of(block * T, T), T)]

    def dev(self, dz, dx, core):
        return ((((self.z + dz + NZ) % NZ) * NX + (self.x + dx) % NX) * 2 + core, self.m)

    def send(self, ref, dz, dx, to_z, to_x, recv, send_sem):
        part = self.rows(ref, dz, dx, self.c)
        copy = pltpu.make_async_remote_copy(
            src_ref=part, dst_ref=part, send_sem=send_sem, recv_sem=recv,
            device_id=self.dev(to_z, to_x, self.c), device_id_type=MESH,
        )
        copy.start()
        self.sent.append(copy)

    def a_z(self, dz, dx, way):
        self.send(self.a, dz, dx, way, 0, self.ra.at[(dz - way) % NZ, dx % NX], self.sza.at[dz % NZ, dx % NX, (way + 1) // 2])

    def a_x(self, to_x):
        self.send(self.a, 0, 0, 0, to_x, self.ra.at[0, (-to_x) % NX], self.sxa.at[to_x])

    def b_z(self, dz, way):
        self.send(self.b, dz, 0, way, 0, self.rb.at[(dz - way) % NZ, 0], self.szb.at[dz % NZ, (way + 1) // 2])

    def b_z_far(self):
        self.send(self.b, -3 * self.dir, 0, self.dir, 0, self.rb.at[4, 0], self.szb.at[3, 0])

    def b_x(self, dz, dx, way):
        self.send(self.b, dz, dx, 0, way, self.rb.at[dz % NZ, (dx - way) % NX], self.sxb.at[dz % NZ, dx % NX, (way + 1) // 2])

    def sib(self, which, dz, dx):
        ref, recv, ssem = (self.a, self.ca, self.sca) if which == 0 else (self.b, self.cb, self.scb)
        part = self.rows(ref, dz, dx, self.c)
        copy = pltpu.make_async_remote_copy(
            src_ref=part, dst_ref=part, send_sem=ssem.at[dz % NZ, dx % NX], recv_sem=recv.at[dz % NZ, dx % NX],
            device_id=self.dev(0, 0, 1 - self.c), device_id_type=MESH,
        )
        copy.start()
        self.sent.append(copy)

    def wait(self, which, dz, dx):
        ref, recv = (self.a, self.ra) if which == 0 else (self.b, self.rb)
        part = self.rows(ref, dz, dx, self.c)
        pltpu.make_async_remote_copy(
            src_ref=part, dst_ref=part, send_sem=self.sxa.at[0], recv_sem=recv.at[dz % NZ, dx % NX],
            device_id=self.dev(0, 0, 1 - self.c), device_id_type=MESH,
        ).wait_recv()

    def wait_sib(self, which, dz, dx):
        ref, recv = (self.a, self.ca) if which == 0 else (self.b, self.cb)
        part = self.rows(ref, dz, dx, 1 - self.c)
        pltpu.make_async_remote_copy(
            src_ref=part, dst_ref=part, send_sem=self.sxa.at[0], recv_sem=recv.at[dz % NZ, dx % NX],
            device_id=self.dev(0, 0, 1 - self.c), device_id_type=MESH,
        ).wait_recv()

    def start_a(self):
        for to_x in (1, 3, 2):
            self.a_x(to_x)
        for way in (1, -1):
            self.a_z(0, 0, way)
        self.sib(0, 0, 0)

    def start_b(self):
        for way in (1, -1):
            self.b_z(0, way)
        for way in (1, -1):
            self.b_x(0, 0, way)
        self.sib(1, 0, 0)

    def first(self):
        for dx in (1, 3, 2):
            self.wait(0, 0, dx)
            for way in (1, -1):
                self.a_z(0, dx, way)
            self.sib(0, 0, dx)
            yield

    def round(self, k):
        if k <= 4:
            for dz in DIST[k]:
                self.wait(1, dz, 0)
                if k < 3:
                    self.b_z(dz, -1 if dz > 0 else 1)
                for way in (1, -1):
                    self.b_x(dz, 0, way)
                self.sib(1, dz, 0)
                yield
            if k == 3:
                self.b_z_far()
        if 1 <= k <= 5:
            for dz in DIST[k - 1]:
                for dx in (1, 3):
                    self.wait(1, dz, dx)
                    if dz % 2 == 0 and dx == 3:
                        self.b_x(dz, dx, 1)
                    if dz % 2 == 1 and dx == 1:
                        self.b_x(dz, dx, -1)
                    self.sib(1, dz, dx)
                    yield
        if 2 <= k <= 6:
            for dz in DIST[k - 2]:
                self.wait(1, dz, 2)
                self.sib(1, dz, 2)
                yield
        if k <= 4:
            for dx in (0, 1, 3, 2):
                for dz in DIST[k]:
                    self.wait(0, dz, dx)
                    way = -1 if dz > 0 else 1
                    if k < 3 or (k == 3 and way == (1 if dx % 2 == 0 else -1)):
                        self.a_z(dz, dx, way)
                    self.sib(0, dz, dx)
                    yield

    def finish(self):
        for copy in self.sent:
            copy.wait_send()


def drain(steps):
    for _ in steps:
        pass


def kernel(
    frames, ids_in, gain, wq, wk, wv, bq, bk, bv, freq, out,
    fs, a2a_src, a2a_dst, ids_buf, ids_dense, ids_t, tok, wa, wb, kbuf, vbuf, qs, acc, mx, den,
    sa_s, sa_r, si_s, si_r, sy_s, sy_r, sp_s, sp_r, se,
    *gsems,
):
    s = lax.axis_index("seq")
    m = lax.axis_index("mp")
    z, x, c = s // (NX * 2), (s // 2) % NX, s % 2
    wg = Gather(wa, wb, gsems[:10], z, x, c, m)
    kg = Gather(kbuf, vbuf, gsems[10:], z, x, c, m)
    sent = []

    barrier = pltpu.get_barrier_semaphore()

    @pl.loop(1, NS)
    def _(k):
        pl.semaphore_signal(barrier, inc=1, device_id=((s + k) % NS, m), device_id_type=MESH)

    @pl.loop(1, NM)
    def _(k):
        pl.semaphore_signal(barrier, inc=1, device_id=(s, (m + k) % NM), device_id_type=MESH)

    for j in range(8):
        fs[pl.ds(j, T, stride=8), :] = frames[:, j * 128:(j + 1) * 128].astype(jnp.float32)
    a2a_src[...] = fs[...].astype(jnp.bfloat16)
    own = pl.ds(pl.multiple_of(s * T, T), T)
    head_cols = pl.ds(pl.multiple_of((m // 2) * HD, HD), HD)
    is_key = m % 2 == 0
    wa[own, :] = wq[:, 0:CA]
    wb[own, 0:512 - CA] = wq[:, CA:512]

    @pl.when(is_key)
    def _():
        wb[own, 512 - CA:CB] = wk[:, head_cols]

    @pl.when(jnp.logical_not(is_key))
    def _():
        wb[own, 512 - CA:CB] = wv[:, head_cols]

    def block16(ref, index):
        return ref.at[pl.ds(pl.multiple_of(index * 16, 16), 16)]

    mine16 = pl.ds(pl.multiple_of(s * 16, 16), 16)
    a2a_dst[mine16, :] = a2a_src[mine16, :]
    ids_buf[pl.ds(s, 1)] = ids_in[pl.ds(s, 1)]
    pl.semaphore_wait(barrier, NS - 1 + NM - 1)

    def a2a_copy(dst_dev, src_block, dst_block, k):
        return pltpu.make_async_remote_copy(
            src_ref=block16(a2a_src, src_block), dst_ref=block16(a2a_dst, dst_block),
            send_sem=sa_s.at[k], recv_sem=sa_r.at[k], device_id=(dst_dev, m), device_id_type=MESH,
        )

    @pl.loop(1, NS)
    def _(k):
        a2a_copy((s + k) % NS, (s + k) % NS, s, k).start()

    wg.start_b()
    wg.start_a()

    def id_copy(dst_dev, src_block, dst_block, send_k, recv_k):
        return pltpu.make_async_remote_copy(
            src_ref=ids_in.at[src_block], dst_ref=ids_buf.at[dst_block],
            send_sem=si_s.at[send_k], recv_sem=si_r.at[recv_k], device_id=(dst_dev, m), device_id_type=MESH,
        )

    @pl.loop(0, NZ)
    def _(k):
        target = k * 8 + m

        @pl.when(target != s)
        def _():
            id_copy(target, target, s, k, s).start()

    drain(wg.first())

    @pl.loop(1, NS)
    def _(k):
        a2a_copy((s + k) % NS, (s + k) % NS, (s - k + NS) % NS, k).wait_recv()

    fs[...] = a2a_dst[...].astype(jnp.float32)
    for j in range(8):
        tok[m, :, j * 128:(j + 1) * 128] = fs[pl.ds(j, T, stride=8), :].astype(jnp.bfloat16)

    def y_copy(d, half, way):
        part = tok.at[(m + d + NM) % NM, pl.ds(half * 64, 64)]
        return pltpu.make_async_remote_copy(
            src_ref=part, dst_ref=part, send_sem=sy_s.at[d % NM, half, (way + 1) // 2],
            recv_sem=sy_r.at[(d - way) % NM, half], device_id=(s, (m + way + NM) % NM), device_id_type=MESH,
        )

    def y_send(d, half, way):
        copy = y_copy(d, half, way)
        copy.start()
        sent.append(copy)

    def y_wait(d, half):
        part = tok.at[(m + d + NM) % NM, pl.ds(half * 64, 64)]
        pltpu.make_async_remote_copy(
            src_ref=part, dst_ref=part, send_sem=sy_s.at[0, 0, 0], recv_sem=sy_r.at[d % NM, half],
            device_id=(s, (m + 1) % NM), device_id_type=MESH,
        ).wait_recv()

    for half in (0, 1):
        for way in (1, -1):
            y_send(0, half, way)

    def y_steps():
        for k in (1, 2, 3, 4):
            for half in (0, 1):
                for d in DIST[k]:
                    y_wait(d, half)
                    way = -1 if d > 0 else 1
                    if k < 3 or (k == 3 and way == (1 if half == 0 else -1)):
                        y_send(d, half, way)
                    yield

    def p_copy(way_k, recv_k):
        return pltpu.make_async_remote_copy(
            src_ref=ids_t, dst_ref=ids_t, send_sem=sp_s.at[way_k], recv_sem=sp_r.at[recv_k],
            device_id=(s, (m + way_k) % NM), device_id_type=MESH,
        )

    collector = s % NM == m

    @pl.when(collector)
    def _():
        @pl.loop(0, NS)
        def _(src):
            @pl.when(src != s)
            def _():
                id_copy((s + 1) % NS, 0, src, 0, src).wait_recv()

        for src in range(NS):
            ids_dense[2 * src:2 * src + 2, :] = ids_buf[src]
        ids_t[...] = ids_dense[...].T[0:8, :]

        @pl.loop(1, NM)
        def _(k):
            p_copy(k, 0).start()

    yield_y = y_steps()
    count = 0
    for k in range(1, 7):
        for _ in wg.round(k):
            count += 1
            if count % 3 == 0:
                next(yield_y, None)
    drain(yield_y)

    @pl.when(jnp.logical_not(collector))
    def _():
        p_copy(1, 0).wait_recv()

    lane = lax.broadcasted_iota(jnp.int32, (T, HD), 1) % (HD // 2)
    columns = jnp.concatenate([ids_t[...], jnp.zeros((HD - 8, T), jnp.float32)], axis=0).T
    chosen = jnp.where(lane < 16, columns[:, 0:1], jnp.where(lane < 40, columns[:, 1:2], columns[:, 2:3]))
    angle = chosen * freq[...]
    cosine = jnp.cos(angle)
    sines = jnp.sin(angle)
    signed = jnp.where(lax.broadcasted_iota(jnp.int32, (T, HD), 1) < HD // 2, -sines, sines)

    squares = jnp.zeros((T, 1), jnp.float32)
    for b in range(NM):
        block = tok[b].astype(jnp.float32)
        squares = squares + jnp.sum(block * block, axis=1, keepdims=True)
    inverse = lax.rsqrt(squares / (NM * 1024.0) + 1e-06)
    for dz in range(NZ):
        for dx in range(NX):
            wg.wait_sib(0, dz, dx)
            wg.wait_sib(1, dz, dx)

    def project(b, carry):
        qa, qb = carry
        at = pl.ds(pl.multiple_of(b * 1024, 1024), 1024)
        normed = (tok[b].astype(jnp.float32) * inverse * gain[:, at].astype(jnp.float32)).astype(jnp.bfloat16)
        qa = qa + jnp.dot(normed, wa[at, :], preferred_element_type=jnp.float32)
        qb = qb + jnp.dot(normed, wb[at, :], preferred_element_type=jnp.float32)
        return qa, qb

    qa, qb = lax.fori_loop(
        0, NM, project, (jnp.zeros((T, CA), jnp.float32), jnp.zeros((T, CB), jnp.float32))
    )

    def rotate(part):
        return (part * cosine + pltpu.roll(part, HD // 2, axis=1) * signed).astype(jnp.bfloat16)

    kv = qb[:, 512 - CA:CB]

    def exchange(ref):
        part = ref.at[own]
        return pltpu.make_async_remote_copy(
            src_ref=part, dst_ref=part, send_sem=se.at[0], recv_sem=se.at[1],
            device_id=(s, m + 1 - 2 * (m % 2)), device_id_type=MESH,
        )

    @pl.when(is_key)
    def _():
        kbuf[own, :] = rotate(kv + bk[:, head_cols].astype(jnp.float32))
        exchange(kbuf).start()

    @pl.when(jnp.logical_not(is_key))
    def _():
        vbuf[own, :] = (kv + bv[:, head_cols].astype(jnp.float32)).astype(jnp.bfloat16)
        exchange(vbuf).start()

    for h in range(4):
        part = qa[:, h * HD:(h + 1) * HD] if h * HD < CA else qb[:, h * HD - CA:(h + 1) * HD - CA]
        qs[h] = rotate(part + bq[:, h * HD:(h + 1) * HD].astype(jnp.float32))
    acc[...] = jnp.zeros_like(acc)
    den[...] = jnp.zeros_like(den)
    mx[...] = jnp.full(mx.shape, -1e30, jnp.float32)

    exchange(kbuf).wait_recv()
    exchange(kbuf).wait_send()
    kg.start_a()
    kg.start_b()

    def slab_body(first_row, masked):
        at = pl.ds(pl.multiple_of(first_row, 1024), 1024)

        @pl.loop(0, 4)
        def _(h):
            scores = lax.dot_general(
                qs[h], kbuf[at, :], (((1,), (1,)), ((), ())), preferred_element_type=jnp.float32
            )
            if masked:
                row = lax.broadcasted_iota(jnp.int32, scores.shape, 0) + (x * 2 + c) * T
                visible = lax.broadcasted_iota(jnp.int32, scores.shape, 1) <= row
                scores = jnp.where(visible, scores, -1e30)
            old = mx[h][:, 0:1]
            new = jnp.maximum(old, jnp.max(scores, axis=1, keepdims=True))
            factor = jnp.exp2((old - new) * EXP_SCALE)
            terms = jnp.exp2((scores - new) * EXP_SCALE)
            if masked:
                terms = jnp.where(visible, terms, 0.0)
            total = den[h][:, 0:1] * factor + jnp.sum(terms, axis=1, keepdims=True)
            acc[h] = acc[h] * factor + jnp.dot(
                terms.astype(jnp.bfloat16), vbuf[at, :], preferred_element_type=jnp.float32
            )
            mx[h] = jnp.broadcast_to(new, (T, HD))
            den[h] = jnp.broadcast_to(total, (T, HD))

    def slab(dz):
        for dx in range(NX):
            kg.wait_sib(0, dz, dx)
            kg.wait_sib(1, dz, dx)
        if dz == 0:
            slab_body(z * 1024, True)
        else:
            zz = (z + dz + NZ) % NZ

            @pl.when(zz < z)
            def _():
                slab_body(zz * 1024, False)

    drain(kg.first())
    for k in range(1, 7):
        drain(kg.round(k))
        if k >= 2:
            for dz in DIST[k - 2]:
                slab(dz)

    for h in range(4):
        out[:, h * HD:(h + 1) * HD] = (acc[h] / den[h]).astype(jnp.bfloat16)

    @pl.loop(1, NS)
    def _(k):
        a2a_copy((s + k) % NS, (s + k) % NS, s, k).wait_send()

    @pl.loop(0, NZ)
    def _(k):
        target = k * 8 + m

        @pl.when(target != s)
        def _():
            id_copy(target, target, s, k, s).wait_send()

    @pl.when(collector)
    def _():
        @pl.loop(1, NM)
        def _(k):
            p_copy(k, 0).wait_send()

    for copy in sent:
        copy.wait_send()
    wg.finish()
    kg.finish()


def gather_sems():
    dma = pltpu.SemaphoreType.DMA
    return [
        dma((NZ, NX)), dma((NZ, NX)), dma((NZ, NX)), dma((NZ, NX)),
        dma((NZ, NX, 2)), dma((NX,)), dma((NZ, 2)), dma((NZ, NX, 2)), dma((NZ, NX)), dma((NZ, NX)),
    ]


def shards(frames_tokens, positions, norm_gain, w_query, w_key, w_value, b_query, b_key, b_value):
    dma = pltpu.SemaphoreType.DMA
    ids = jnp.pad(positions.astype(jnp.float32).reshape(NS, 2, 3), ((0, 0), (0, 0), (0, HD - 3)))
    half = np.power(1000000.0, -(2.0 * np.arange(HD // 2)) / HD).astype(np.float32)
    freq = jnp.asarray(np.concatenate([half, half])[None, :])
    vmem = pl.BlockSpec(memory_space=pltpu.VMEM)
    return pl.pallas_call(
        kernel,
        name="fused",
        out_shape=jax.ShapeDtypeStruct((T, 512), jnp.bfloat16),
        in_specs=[vmem] * 10,
        out_specs=vmem,
        scratch_shapes=[
            pltpu.VMEM((1024, 128), jnp.float32),
            pltpu.VMEM((1024, 128), jnp.bfloat16),
            pltpu.VMEM((1024, 128), jnp.bfloat16),
            pltpu.VMEM((NS, 2, HD), jnp.float32),
            pltpu.VMEM((T, HD), jnp.float32),
            pltpu.VMEM((8, T), jnp.float32),
            pltpu.VMEM((NM, T, 1024), jnp.bfloat16),
            pltpu.VMEM((NS * T, CA), jnp.bfloat16),
            pltpu.VMEM((NS * T, CB), jnp.bfloat16),
            pltpu.VMEM((NS * T, HD), jnp.bfloat16),
            pltpu.VMEM((NS * T, HD), jnp.bfloat16),
            pltpu.VMEM((4, T, HD), jnp.bfloat16),
            pltpu.VMEM((4, T, HD), jnp.float32),
            pltpu.VMEM((4, T, HD), jnp.float32),
            pltpu.VMEM((4, T, HD), jnp.float32),
            dma((NS,)), dma((NS,)), dma((NZ,)), dma((NS,)),
            dma((NM, 2, 2)), dma((NM, 2)), dma((NM,)), dma((1,)), dma((2,)),
        ] + gather_sems() + gather_sems(),
        compiler_params=pltpu.CompilerParams(
            collective_id=0, has_side_effects=True, vmem_limit_bytes=52 * 2**20
        ),
        cost_estimate=pl.CostEstimate(flops=5 * 10**9, bytes_accessed=10**7, transcendentals=4 * 10**6),
    )(
        frames_tokens, ids, norm_gain[None, :], w_query, w_key, w_value,
        b_query[None, :], b_key[None, :], b_value[None, :], freq,
    )


def solution(mesh):
    in_specs = (
        P("seq", "mp"), P("seq", None), P(), P("seq", "mp"), P("seq", None), P("seq", None),
        P("mp"), P(), P(),
    )
    return jax.shard_map(shards, mesh=mesh, in_specs=in_specs, out_specs=P("seq", "mp"), check_vma=False)
```

```python
import functools
import math

import jax
import jax.numpy as jnp
import numpy as np
from jax import lax
from jax.experimental import pallas as pl
from jax.experimental.pallas import tpu as pltpu
from jax.sharding import PartitionSpec as P

HD = 128
T = 128
NX, NZ, NM = 4, 8, 8
NS = NZ * NX * 2
CA, CB = 256, 384
MESH = pl.DeviceIdType.MESH
DIST = [[0], [-1, 1], [-2, 2], [-3, 3], [4]]
EXP_SCALE = math.log2(math.e) / math.sqrt(HD)


class Gather:
    def __init__(self, a, b, sems, z, x, c, m, direct_b):
        self.a, self.b = a, b
        self.ra, self.rb, self.ca, self.cb, self.sa, self.sb = sems
        self.z, self.x, self.c, self.m = z, x, c, m
        self.dir = 1 - 2 * c
        self.direct_b = direct_b

    def rows(self, ref, dz, dx, core):
        block = (core * NZ + (self.z + dz + NZ) % NZ) * NX + (self.x + dx) % NX
        return ref.at[pl.ds(pl.multiple_of(block * T, T), T)]

    def four(self, ref, dz, core):
        first = (core * NZ + (self.z + dz + NZ) % NZ) * NX
        return ref.at[pl.ds(pl.multiple_of(first * T, NX * T), NX * T)]

    def dev(self, dz, dx, core):
        return ((((self.z + dz + NZ) % NZ) * NX + (self.x + dx) % NX) * 2 + core, self.m)

    def copy(self, part, send_sem, recv_sem, device):
        return pltpu.make_async_remote_copy(
            src_ref=part, dst_ref=part, send_sem=send_sem, recv_sem=recv_sem,
            device_id=device, device_id_type=MESH,
        )

    def send(self, ref, dz, dx, to_z, to_x, recv, send_sem):
        self.copy(self.rows(ref, dz, dx, self.c), send_sem, recv, self.dev(to_z, to_x, self.c)).start()

    def a_z(self, dz, dx, way):
        self.send(self.a, dz, dx, way, 0, self.ra.at[(dz - way) % NZ, dx % NX], self.sa.at[0])

    def a_x(self, to_x):
        self.send(self.a, 0, 0, 0, to_x, self.ra.at[0, (-to_x) % NX], self.sa.at[0])

    def b_z(self, dz, way):
        self.send(self.b, dz, 0, way, 0, self.rb.at[(dz - way) % NZ, 0], self.sb.at[0])

    def b_z_far(self):
        self.send(self.b, -3 * self.dir, 0, self.dir, 0, self.rb.at[4, 0], self.sb.at[0])

    def b_x(self, dz):
        for to_x in (1, 3, 2):
            self.send(self.b, dz, 0, 0, to_x, self.rb.at[dz % NZ, (-to_x) % NX], self.sb.at[0])

    def sib(self, which, dz):
        ref, recv, send = (self.a, self.ca, self.sa) if which == 0 else (self.b, self.cb, self.sb)
        self.copy(self.four(ref, dz, self.c), send.at[1], recv.at[dz % NZ], self.dev(0, 0, 1 - self.c)).start()

    def wait(self, which, dz, dx):
        ref, recv, send = (self.a, self.ra, self.sa) if which == 0 else (self.b, self.rb, self.sb)
        self.copy(
            self.rows(ref, dz, dx, self.c), send.at[0], recv.at[dz % NZ, dx % NX], self.dev(0, 0, 1 - self.c)
        ).wait_recv()

    def wait_sib(self, which, dz):
        ref, recv, send = (self.a, self.ca, self.sa) if which == 0 else (self.b, self.cb, self.sb)
        self.copy(
            self.four(ref, dz, 1 - self.c), send.at[1], recv.at[dz % NZ], self.dev(0, 0, 1 - self.c)
        ).wait_recv()

    def start_a(self):
        for to_x in (1, 3, 2):
            self.a_x(to_x)
        for way in (1, -1):
            self.a_z(0, 0, way)

    def start_b(self):
        for way in (1, -1, 2, -2, 3, -3, 4) if self.direct_b else (1, -1):
            self.b_z(0, way)
        self.b_x(0)

    def first(self):
        for dx in (1, 3, 2):
            self.wait(0, 0, dx)
            for way in (1, -1):
                self.a_z(0, dx, way)
            yield
        self.sib(0, 0)

    def b_arrive(self, k):
        for dz in DIST[k]:
            self.wait(1, dz, 0)
            if k < 3 and not self.direct_b:
                self.b_z(dz, -1 if dz > 0 else 1)
            self.b_x(dz)
            yield
        if k == 3 and not self.direct_b:
            self.b_z_far()

    def b_across(self, k):
        for dz in DIST[k]:
            for dx in (1, 3, 2):
                self.wait(1, dz, dx)
            self.sib(1, dz)
            yield

    def a_arrive(self, k):
        for dx in (0, 1, 3, 2):
            for dz in DIST[k]:
                self.wait(0, dz, dx)
                way = -1 if dz > 0 else 1
                if k < 3 or (k == 3 and way == (1 if dx % 2 == 0 else -1)):
                    self.a_z(dz, dx, way)
                yield
        for dz in DIST[k]:
            self.sib(0, dz)

    def finish(self):
        for ref, send in ((self.a, self.sa), (self.b, self.sb)):
            for k, count in ((0, 31), (1, 32)):
                self.copy(ref.at[pl.ds(0, count * T)], send.at[k], send.at[k], self.dev(0, 0, 1 - self.c)).wait_send()


def drain(steps):
    for _ in steps:
        pass


def kernel(
    frames_in, ids_hbm, gain_hbm, wq, wk, wv, bq_hbm, bk_hbm, bv_hbm, freq_hbm, out,
    frames, ids_in, gain, bq, bk, bv, freq, fs, a2a_src, a2a_dst, ids_src, ids_buf, ids_dense, ids_t, tok, nrm, wa, wb, kv, qs, acc, mx, den,
    squares, tables, biases, s_in, sa_s, sa_r, si_s, si_r, sy_s, sy_r, sp_s, sp_r, se,
    *gsems,
):
    s = lax.axis_index("seq")
    m = lax.axis_index("mp")
    z, x, c = s // (NX * 2), (s // 2) % NX, s % 2
    wg = Gather(wa, wb, gsems[:6], z, x, c, m, False)
    own_kind, other_kind = kv.at[pl.ds(0, NS * T)], kv.at[pl.ds(NS * T, NS * T)]
    kg = Gather(other_kind, own_kind, gsems[6:], z, x, c, m, True)

    barrier = pltpu.get_barrier_semaphore()

    block = (c * NZ + z) * NX + x
    own = pl.ds(pl.multiple_of(block * T, T), T)
    head_cols = pl.ds(pl.multiple_of((m // 2) * HD, HD), HD)
    is_key = m % 2 == 0
    load_frames = pltpu.make_async_copy(frames_in, frames, s_in.at[0])
    load_qa = pltpu.make_async_copy(wq.at[:, pl.ds(0, CA)], wa.at[own], s_in.at[1])
    load_qb = pltpu.make_async_copy(wq.at[:, pl.ds(CA, 512 - CA)], wb.at[own, pl.ds(0, 512 - CA)], s_in.at[2])
    load_k = pltpu.make_async_copy(wk.at[:, head_cols], wb.at[own, pl.ds(512 - CA, HD)], s_in.at[3])
    load_v = pltpu.make_async_copy(wv.at[:, head_cols], wb.at[own, pl.ds(512 - CA, HD)], s_in.at[3])
    small = [
        pltpu.make_async_copy(src, dst, s_in.at[4 + k])
        for k, (src, dst) in enumerate(
            ((ids_hbm, ids_in), (gain_hbm, gain), (bq_hbm, bq), (bk_hbm, bk), (bv_hbm, bv), (freq_hbm, freq))
        )
    ]
    load_frames.start()
    for copy in small:
        copy.start()
    load_qa.start()
    load_qb.start()

    @pl.when(is_key)
    def _():
        load_k.start()

    @pl.when(jnp.logical_not(is_key))
    def _():
        load_v.start()

    @pl.loop(1, NS)
    def _(k):
        pl.semaphore_signal(barrier, inc=1, device_id=((s + k) % NS, m), device_id_type=MESH)

    @pl.loop(1, NM)
    def _(k):
        pl.semaphore_signal(barrier, inc=1, device_id=(s, (m + k) % NM), device_id_type=MESH)

    def block16(ref, index):
        return ref.at[pl.ds(pl.multiple_of(index * 16, 16), 16)]

    mine16 = pl.ds(pl.multiple_of(s * 16, 16), 16)
    load_frames.wait()
    for copy in small:
        copy.wait()
    for j in range(8):
        fs[pl.ds(j, T, stride=8), :] = frames[:, j * 128:(j + 1) * 128].astype(jnp.float32)
    a2a_src[...] = fs[...].astype(jnp.bfloat16)
    a2a_dst[mine16, :] = a2a_src[mine16, :]
    ids_rows = jnp.concatenate([ids_in[...].astype(jnp.float32), jnp.zeros((HD - 3, T), jnp.float32)], axis=0).T
    for k in range(NS):
        ids_src[k] = ids_rows[2 * k:2 * k + 2, :]
    ids_buf[pl.ds(s, 1)] = ids_src[pl.ds(s, 1)]
    for row, ref in enumerate((bq, bk, bv)):
        biases[row:row + 1, :] = ref[...].astype(jnp.float32).reshape(1, 512)
    load_qa.wait()
    load_qb.wait()
    load_k.wait()
    pl.semaphore_wait(barrier, NS - 1 + NM - 1)

    wg.start_b()
    wg.start_a()

    def a2a_copy(dst_dev, src_block, dst_block):
        return pltpu.make_async_remote_copy(
            src_ref=block16(a2a_src, src_block), dst_ref=block16(a2a_dst, dst_block),
            send_sem=sa_s.at[0], recv_sem=sa_r.at[0], device_id=(dst_dev, m), device_id_type=MESH,
        )

    @pl.loop(1, NS)
    def _(k):
        a2a_copy((s + k) % NS, (s + k) % NS, s).start()

    a2a_all = pltpu.make_async_remote_copy(
        src_ref=a2a_src.at[pl.ds(0, (NS - 1) * 16)], dst_ref=a2a_dst.at[pl.ds(0, (NS - 1) * 16)],
        send_sem=sa_s.at[0], recv_sem=sa_r.at[0], device_id=((s + 1) % NS, m), device_id_type=MESH,
    )

    def id_copy(target, k):
        return pltpu.make_async_remote_copy(
            src_ref=ids_src.at[target], dst_ref=ids_buf.at[s],
            send_sem=si_s.at[k], recv_sem=si_r.at[0], device_id=(target, m), device_id_type=MESH,
        )

    @pl.loop(0, NZ)
    def _(k):
        target = k * 8 + m

        @pl.when(target != s)
        def _():
            id_copy(target, k).start()

    drain(wg.first())
    a2a_all.wait_recv()
    fs[...] = a2a_dst[...].astype(jnp.float32)
    for j in range(8):
        tok[m, :, j * 128:(j + 1) * 128] = fs[pl.ds(j, T, stride=8), :].astype(jnp.bfloat16)

    def y_send(d, half, way):
        part = tok.at[(m + d + NM) % NM, pl.ds(half * 64, 64)]
        pltpu.make_async_remote_copy(
            src_ref=part, dst_ref=part, send_sem=sy_s.at[0],
            recv_sem=sy_r.at[(d - way) % NM, half], device_id=(s, (m + way + NM) % NM), device_id_type=MESH,
        ).start()

    def y_wait(d, half):
        part = tok.at[(m + d + NM) % NM, pl.ds(half * 64, 64)]
        pltpu.make_async_remote_copy(
            src_ref=part, dst_ref=part, send_sem=sy_s.at[0], recv_sem=sy_r.at[d % NM, half],
            device_id=(s, (m + 1) % NM), device_id_type=MESH,
        ).wait_recv()

    for half in (0, 1):
        for way in (1, -1):
            y_send(0, half, way)

    squares[...] = jnp.zeros_like(squares)

    def add_squares(d, half):
        rows = pl.ds(half * 64, 64)
        total = squares[rows, :]
        for j in range(8):
            part = tok[(m + d + NM) % NM, rows, j * 128:(j + 1) * 128].astype(jnp.float32)
            total = total + part * part
        squares[rows, :] = total

    for half in (0, 1):
        add_squares(0, half)

    def y_steps():
        for k in (1, 2, 3, 4):
            for half in (0, 1):
                for d in DIST[k]:
                    y_wait(d, half)
                    way = -1 if d > 0 else 1
                    if k < 3 or (k == 3 and way == (1 if half == 0 else -1)):
                        y_send(d, half, way)
                    add_squares(d, half)
                    yield

    def p_copy(way_k):
        return pltpu.make_async_remote_copy(
            src_ref=ids_t, dst_ref=ids_t, send_sem=sp_s.at[way_k],
            recv_sem=sp_r.at[0], device_id=(s, (m + way_k) % NM), device_id_type=MESH,
        )

    collector = s % NM == m

    def collect_ids():
        @pl.when(collector)
        def _():
            pltpu.make_async_remote_copy(
                src_ref=ids_src.at[pl.ds(0, NS - 1)], dst_ref=ids_buf.at[pl.ds(0, NS - 1)],
                send_sem=si_s.at[0], recv_sem=si_r.at[0], device_id=((s + 1) % NS, m), device_id_type=MESH,
            ).wait_recv()
            for src in range(NS):
                ids_dense[2 * src:2 * src + 2, :] = ids_buf[src]
            ids_t[...] = ids_dense[...].T[0:8, :]

            @pl.loop(1, NM)
            def _(k):
                p_copy(k).start()

    def make_tables():
        @pl.when(jnp.logical_not(collector))
        def _():
            p_copy(1).wait_recv()

        lane = lax.broadcasted_iota(jnp.int32, (T, HD), 1)
        front = lane < HD // 2
        place = jnp.where(front, lane, lane - HD // 2)
        columns = jnp.concatenate([ids_t[...], jnp.zeros((HD - 8, T), jnp.float32)], axis=0).T
        chosen = jnp.where(place < 16, columns[:, 0:1], jnp.where(place < 40, columns[:, 1:2], columns[:, 2:3]))
        angle = chosen * freq[...]
        sines = jnp.sin(angle)
        tables[0] = jnp.cos(angle)
        tables[1] = jnp.where(front, -sines, sines)

    def weight_steps():
        yield from wg.b_arrive(1)
        yield from wg.b_across(0)
        yield from wg.a_arrive(1)
        collect_ids()
        yield from wg.b_arrive(2)
        yield from wg.b_across(1)
        yield from wg.a_arrive(2)
        yield from wg.b_arrive(3)
        yield from wg.b_across(2)
        yield from wg.a_arrive(3)
        make_tables()
        yield from wg.b_arrive(4)
        yield from wg.b_across(3)
        yield from wg.a_arrive(4)
        yield from wg.b_across(4)

    ring = y_steps()
    for index, _ in enumerate(weight_steps()):
        if index >= 4 and index % 5 < 2:
            next(ring, None)
    drain(ring)

    inverse = lax.rsqrt(jnp.sum(squares[...], axis=1, keepdims=True) / (NM * 1024.0) + 1e-06)
    acc[...] = jnp.zeros_like(acc)
    den[...] = jnp.zeros_like(den)
    mx[...] = jnp.full(mx.shape, -1e30, jnp.float32)
    for dz in range(NZ):
        wg.wait_sib(0, dz)
        wg.wait_sib(1, dz)

    def of_core(block, core):
        cols = [block[:, (k * 2 + core) * T:(k * 2 + core + 1) * T] for k in range(NX)]
        return jnp.concatenate(cols, axis=1)

    def core_rows(b, core):
        return pl.ds(pl.multiple_of((core * NZ + b) * NX * T, NX * T), NX * T)

    def project_kv(b, total):
        at = pl.ds(pl.multiple_of(b * 1024, 1024), 1024)
        scale = gain[at].astype(jnp.float32).reshape(1, 1024)
        normed = (tok[b].astype(jnp.float32) * inverse * scale).astype(jnp.bfloat16)
        nrm[b] = normed
        for core in (0, 1):
            total = total + jnp.dot(
                of_core(normed, core), wb[core_rows(b, core), 512 - CA:CB], preferred_element_type=jnp.float32
            )
        return total

    linear = lax.fori_loop(0, NM, project_kv, jnp.zeros((T, HD), jnp.float32))

    def rotate(part):
        return part * tables[0] + pltpu.roll(part, HD // 2, axis=1) * tables[1]

    linear = linear + jnp.where(is_key, biases[1:2, head_cols], biases[2:3, head_cols])
    own_kind[own, :] = jnp.where(is_key, rotate(linear), linear).astype(jnp.bfloat16)

    exchange = pltpu.make_async_remote_copy(
        src_ref=own_kind.at[own], dst_ref=other_kind.at[own], send_sem=se.at[0], recv_sem=se.at[1],
        device_id=(s, m + 1 - 2 * (m % 2)), device_id_type=MESH,
    )
    exchange.start()
    kg.start_b()

    def project_q(b, carry):
        qa, qb = carry
        for core in (0, 1):
            rows = core_rows(b, core)
            part = of_core(nrm[b], core)
            qa = qa + jnp.dot(part, wa[rows, :], preferred_element_type=jnp.float32)
            qb = qb + jnp.dot(part, wb[rows, 0:512 - CA], preferred_element_type=jnp.float32)
        return qa, qb

    zeros = jnp.zeros((T, CA), jnp.float32)
    qa, qb = lax.fori_loop(0, NM, project_q, (zeros, zeros))
    exchange.wait_recv()
    kg.start_a()

    for h in range(4):
        part = (qa, qb)[h // 2][:, (h % 2) * HD:(h % 2 + 1) * HD]
        qs[h] = rotate(part + biases[0:1, h * HD:(h + 1) * HD]).astype(jnp.bfloat16)

    key_base = jnp.where(is_key, 0, NS * T)

    def slab_body(zz, masked):
        def rows_of(base, core):
            return pl.ds(pl.multiple_of(base + (core * NZ + zz) * NX * T, NX * T), NX * T)

        @pl.loop(0, 4)
        def _(h):
            scores = jnp.concatenate(
                [
                    lax.dot_general(
                        qs[h], kv[rows_of(key_base, core), :], (((1,), (1,)), ((), ())),
                        preferred_element_type=jnp.float32,
                    )
                    for core in (0, 1)
                ],
                axis=1,
            )
            if masked:
                row = lax.broadcasted_iota(jnp.int32, scores.shape, 0) + (x * 2 + c) * T
                lane = lax.broadcasted_iota(jnp.int32, scores.shape, 1)
                blk = lane // T
                key = jnp.where(blk < NX, blk * 2, (blk - NX) * 2 + 1) * T + (lane - blk * T)
                visible = key <= row
                scores = jnp.where(visible, scores, -1e30)
            old = mx[h][:, 0:1]
            new = jnp.maximum(old, jnp.max(scores, axis=1, keepdims=True))
            factor = jnp.exp2((old - new) * EXP_SCALE)
            terms = jnp.exp2((scores - new) * EXP_SCALE)
            if masked:
                terms = jnp.where(visible, terms, 0.0)
            total = den[h][:, 0:1] * factor + jnp.sum(terms, axis=1, keepdims=True)
            probs = terms.astype(jnp.bfloat16)
            mixed = acc[h] * factor
            for core in (0, 1):
                mixed = mixed + jnp.dot(
                    probs[:, core * NX * T:(core + 1) * NX * T], kv[rows_of(NS * T - key_base, core), :],
                    preferred_element_type=jnp.float32,
                )
            acc[h] = mixed
            mx[h] = jnp.broadcast_to(new, (T, HD))
            den[h] = jnp.broadcast_to(total, (T, HD))

    def slab(k):
        for dz in DIST[k]:
            kg.wait_sib(0, dz)
            kg.wait_sib(1, dz)
            if dz == 0:
                slab_body(z, True)
            else:
                zz = (z + dz + NZ) % NZ

                @pl.when(zz < z)
                def _():
                    slab_body(zz, False)

    drain(kg.b_arrive(1))
    drain(kg.first())
    drain(kg.b_arrive(2))
    drain(kg.b_across(0))
    drain(kg.b_arrive(3))
    drain(kg.a_arrive(1))
    drain(kg.b_arrive(4))
    drain(kg.b_across(1))
    slab(0)
    drain(kg.a_arrive(2))
    drain(kg.b_across(2))
    slab(1)
    drain(kg.a_arrive(3))
    drain(kg.b_across(3))
    slab(2)
    drain(kg.a_arrive(4))
    drain(kg.b_across(4))
    slab(3)
    slab(4)

    for h in range(4):
        out[:, h * HD:(h + 1) * HD] = (acc[h] / den[h]).astype(jnp.bfloat16)

    a2a_all.wait_send()

    @pl.loop(0, NZ)
    def _(k):
        target = k * 8 + m

        @pl.when(target != s)
        def _():
            id_copy(target, k).wait_send()

    @pl.when(collector)
    def _():
        @pl.loop(1, NM)
        def _(k):
            p_copy(k).wait_send()

    exchange.wait_send()
    seven = tok.at[pl.ds(0, 7)]
    pltpu.make_async_remote_copy(
        src_ref=seven, dst_ref=seven, send_sem=sy_s.at[0], recv_sem=sy_r.at[0, 0],
        device_id=(s, (m + 1) % NM), device_id_type=MESH,
    ).wait_send()
    wg.finish()
    kg.finish()


def gather_sems():
    dma = pltpu.SemaphoreType.DMA
    return [dma((NZ, NX)), dma((NZ, NX)), dma((NZ,)), dma((NZ,)), dma((2,)), dma((2,))]


def shards(frames_tokens, positions, norm_gain, w_query, w_key, w_value, b_query, b_key, b_value):
    dma = pltpu.SemaphoreType.DMA
    half = np.power(1000000.0, -(2.0 * np.arange(HD // 2)) / HD).astype(np.float32)
    freq = jnp.asarray(np.concatenate([half, half])[None, :])
    vmem = pl.BlockSpec(memory_space=pltpu.VMEM)
    hbm = pl.BlockSpec(memory_space=pltpu.HBM)
    return pl.pallas_call(
        kernel,
        name="fused",
        out_shape=jax.ShapeDtypeStruct((T, 512), jnp.bfloat16),
        in_specs=[hbm] * 10,
        out_specs=vmem,
        scratch_shapes=[
            pltpu.VMEM((T, 1024), jnp.bfloat16),
            pltpu.VMEM((3, T), jnp.int32),
            pltpu.VMEM((NS * T,), jnp.bfloat16),
            pltpu.VMEM((512,), jnp.bfloat16),
            pltpu.VMEM((512,), jnp.bfloat16),
            pltpu.VMEM((512,), jnp.bfloat16),
            pltpu.VMEM((1, HD), jnp.float32),
            pltpu.VMEM((1024, 128), jnp.float32),
            pltpu.VMEM((1024, 128), jnp.bfloat16),
            pltpu.VMEM((1024, 128), jnp.bfloat16),
            pltpu.VMEM((NS, 2, HD), jnp.float32),
            pltpu.VMEM((NS, 2, HD), jnp.float32),
            pltpu.VMEM((T, HD), jnp.float32),
            pltpu.VMEM((8, T), jnp.float32),
            pltpu.VMEM((NM, T, 1024), jnp.bfloat16),
            pltpu.VMEM((NM, T, 1024), jnp.bfloat16),
            pltpu.VMEM((NS * T, CA), jnp.bfloat16),
            pltpu.VMEM((NS * T, CB), jnp.bfloat16),
            pltpu.VMEM((2 * NS * T, HD), jnp.bfloat16),
            pltpu.VMEM((4, T, HD), jnp.bfloat16),
            pltpu.VMEM((4, T, HD), jnp.float32),
            pltpu.VMEM((4, T, HD), jnp.float32),
            pltpu.VMEM((4, T, HD), jnp.float32),
            pltpu.VMEM((T, HD), jnp.float32),
            pltpu.VMEM((2, T, HD), jnp.float32),
            pltpu.VMEM((8, 512), jnp.float32),
            dma((10,)), dma((1,)), dma((1,)), dma((NZ,)), dma((1,)),
            dma((1,)), dma((NM, 2)), dma((NM,)), dma((1,)), dma((2,)),
        ] + gather_sems() + gather_sems(),
        compiler_params=pltpu.CompilerParams(
            collective_id=0, has_side_effects=True, vmem_limit_bytes=64 * 2**20 - 2**17
        ),
        cost_estimate=pl.CostEstimate(flops=5 * 10**9, bytes_accessed=10**7, transcendentals=4 * 10**6),
    )(
        frames_tokens, positions.T, norm_gain, w_query, w_key, w_value, b_query, b_key, b_value, freq,
    )


def solution(mesh):
    in_specs = (
        P("seq", "mp"), P("seq", None), P(), P("seq", "mp"), P("seq", None), P("seq", None),
        P("mp"), P(), P(),
    )
    return jax.shard_map(shards, mesh=mesh, in_specs=in_specs, out_specs=P("seq", "mp"), check_vma=False)
```

```python
import functools
import math

import jax
import jax.numpy as jnp
import numpy as np
from jax import lax
from jax.experimental import pallas as pl
from jax.experimental.pallas import tpu as pltpu
from jax.sharding import PartitionSpec as P

HD = 128
T = 128
NX, NZ, NM = 4, 8, 8
NS = NZ * NX * 2
CA, CB = 256, 384
MESH = pl.DeviceIdType.MESH
DIST = [[0], [-1, 1], [-2, 2], [-3, 3], [4]]
EXP_SCALE = math.log2(math.e) / math.sqrt(HD)


class Gather:
    def __init__(self, a, b, sems, z, x, c, m, direct_b):
        self.a, self.b = a, b
        self.ra, self.rb, self.ca, self.cb, self.sa, self.sb = sems
        self.z, self.x, self.c, self.m = z, x, c, m
        self.dir = 1 - 2 * c
        self.direct_b = direct_b
        self.zs = [lax.rem(z + dz, NZ) for dz in range(NZ)]
        self.xs = [lax.rem(x + dx, NX) for dx in range(NX)]

    def rows(self, ref, dz, dx, core):
        block = (core * NZ + self.at_z(dz)) * NX + self.xs[dx % NX]
        return ref.at[pl.ds(pl.multiple_of(block * T, T), T)]

    def four(self, ref, dz, core):
        first = (core * NZ + self.at_z(dz)) * NX
        return ref.at[pl.ds(pl.multiple_of(first * T, NX * T), NX * T)]

    def dev(self, dz, dx, core):
        return ((self.at_z(dz) * NX + self.xs[dx % NX]) * 2 + core, self.m)

    def at_z(self, dz):
        return self.zs[dz % NZ] if isinstance(dz, int) else lax.rem(self.z + dz + NZ, NZ)

    def copy(self, part, send_sem, recv_sem, device):
        return pltpu.make_async_remote_copy(
            src_ref=part, dst_ref=part, send_sem=send_sem, recv_sem=recv_sem,
            device_id=device, device_id_type=MESH,
        )

    def send(self, ref, dz, dx, to_z, to_x, recv, send_sem):
        self.copy(self.rows(ref, dz, dx, self.c), send_sem, recv, self.dev(to_z, to_x, self.c)).start()

    def a_z(self, dz, dx, way):
        self.send(self.a, dz, dx, way, 0, self.ra.at[(dz - way) % NZ, dx % NX], self.sa.at[0])

    def a_x(self, to_x):
        self.send(self.a, 0, 0, 0, to_x, self.ra.at[0, (-to_x) % NX], self.sa.at[0])

    def b_z(self, dz, way):
        self.send(self.b, dz, 0, way, 0, self.rb.at[(dz - way) % NZ, 0], self.sb.at[0])

    def b_z_far(self):
        self.send(self.b, -2 * self.dir, 0, 2 * self.dir, 0, self.rb.at[4, 0], self.sb.at[0])

    def straight(self, dz):
        return self.direct_b or dz == 4

    def b_x(self, dz):
        for to_x in (1, 3, 2) if self.straight(dz) else (1, 3):
            self.send(self.b, dz, 0, 0, to_x, self.rb.at[dz % NZ, (-to_x) % NX], self.sb.at[0])

    def sib(self, which, dz):
        ref, recv, send = (self.a, self.ca, self.sa) if which == 0 else (self.b, self.cb, self.sb)
        self.copy(self.four(ref, dz, self.c), send.at[1], recv.at[dz % NZ], self.dev(0, 0, 1 - self.c)).start()

    def wait(self, which, dz, dx):
        ref, recv, send = (self.a, self.ra, self.sa) if which == 0 else (self.b, self.rb, self.sb)
        self.copy(
            self.rows(ref, dz, dx, self.c), send.at[0], recv.at[dz % NZ, dx % NX], self.dev(0, 0, 1 - self.c)
        ).wait_recv()

    def wait_sib(self, which, dz):
        ref, recv, send = (self.a, self.ca, self.sa) if which == 0 else (self.b, self.cb, self.sb)
        self.copy(
            self.four(ref, dz, 1 - self.c), send.at[1], recv.at[dz % NZ], self.dev(0, 0, 1 - self.c)
        ).wait_recv()

    def start_a(self):
        for to_x in (1, 3, 2):
            self.a_x(to_x)
        for way in (1, -1):
            self.a_z(0, 0, way)

    def start_b(self):
        for way in (1, -1, 2, -2, 3, -3, 4) if self.direct_b else (1, -1, 2, -2):
            self.b_z(0, way)
        self.b_x(0)

    def first(self):
        for dx in (1, 3, 2):
            self.wait(0, 0, dx)
            for way in (1, -1):
                self.a_z(0, dx, way)
            yield
        self.sib(0, 0)

    def b_arrive(self, k):
        for dz in DIST[k]:
            self.wait(1, dz, 0)
            if k == 2 and not self.direct_b:
                self.b_z(dz, -1 if dz > 0 else 1)
            self.b_x(dz)
            yield
        if k == 2 and not self.direct_b:
            self.b_z_far()

    def b_across(self, k):
        for dz in DIST[k]:
            for dx in (1, 3):
                self.wait(1, dz, dx)
                if not self.straight(dz) and dx == (3 if dz % 2 == 0 else 1):
                    way = 1 if dx == 3 else -1
                    self.send(self.b, dz, dx, 0, way, self.rb.at[dz % NZ, 2], self.sb.at[0])
                yield

    def b_last(self, k):
        for dz in DIST[k]:
            self.wait(1, dz, 2)
            self.sib(1, dz)
            yield

    def a_arrive(self, k):
        for dx in (0, 1, 3, 2):
            for dz in DIST[k]:
                self.wait(0, dz, dx)
                way = -1 if dz > 0 else 1
                if k < 3 or (k == 3 and way == (1 if dx % 2 == 0 else -1)):
                    self.a_z(dz, dx, way)
                yield
        for dz in DIST[k]:
            self.sib(0, dz)

    def finish(self):
        for ref, send in ((self.a, self.sa), (self.b, self.sb)):
            for k, count in ((0, 31), (1, 32)):
                self.copy(ref.at[pl.ds(0, count * T)], send.at[k], send.at[k], self.dev(0, 0, 1 - self.c)).wait_send()


def drain(steps):
    for _ in steps:
        pass


def kernel(
    frames_in, ids_hbm, gain_hbm, wq, wk, wv, bq_hbm, bk_hbm, bv_hbm, freq_hbm, out,
    frames, ids_in, gain, bq, bk, bv, freq, fs, a2a_src, a2a_dst, ids_src, ids_buf, ids_dense, ids_t, tok, nrm, wa, wb, kv, qs, acc, mx, den,
    line_a, line_b, inverse, sums_src, sums, tables, biases, s_in, sq_s, sq_r, sa_s, sa_r, si_s, si_r, sy_s, sy_r, sp_s, sp_r, se,
    *gsems,
):
    s = lax.axis_index("seq")
    m = lax.axis_index("mp")
    z, x, c = s // (NX * 2), (s // 2) % NX, s % 2
    wg = Gather(wa, wb, gsems[:6], z, x, c, m, False)
    own_kind, other_kind = kv.at[pl.ds(0, NS * T)], kv.at[pl.ds(NS * T, NS * T)]
    kg = Gather(other_kind, own_kind, gsems[6:], z, x, c, m, True)

    barrier = pltpu.get_barrier_semaphore()

    block = (c * NZ + z) * NX + x
    own = pl.ds(pl.multiple_of(block * T, T), T)
    head_cols = pl.ds(pl.multiple_of((m // 2) * HD, HD), HD)
    is_key = m % 2 == 0
    load_frames = pltpu.make_async_copy(frames_in, frames, s_in.at[0])
    load_qa = pltpu.make_async_copy(wq.at[:, pl.ds(0, CA)], wa.at[own], s_in.at[1])
    load_qb = pltpu.make_async_copy(wq.at[:, pl.ds(CA, 512 - CA)], wb.at[own, pl.ds(0, 512 - CA)], s_in.at[2])
    load_k = pltpu.make_async_copy(wk.at[:, head_cols], wb.at[own, pl.ds(512 - CA, HD)], s_in.at[3])
    load_v = pltpu.make_async_copy(wv.at[:, head_cols], wb.at[own, pl.ds(512 - CA, HD)], s_in.at[3])
    small = [
        pltpu.make_async_copy(src, dst, s_in.at[4 + k])
        for k, (src, dst) in enumerate(
            ((ids_hbm, ids_in), (gain_hbm, gain), (bq_hbm, bq), (bk_hbm, bk), (bv_hbm, bv), (freq_hbm, freq))
        )
    ]
    load_frames.start()
    for copy in small:
        copy.start()
    load_qa.start()
    load_qb.start()

    @pl.when(is_key)
    def _():
        load_k.start()

    @pl.when(jnp.logical_not(is_key))
    def _():
        load_v.start()

    @pl.loop(1, NS)
    def _(k):
        pl.semaphore_signal(barrier, inc=1, device_id=(lax.rem(s + k, NS), m), device_id_type=MESH)

    @pl.loop(1, NM)
    def _(k):
        pl.semaphore_signal(barrier, inc=1, device_id=(s, lax.rem(m + k, NM)), device_id_type=MESH)

    def block16(ref, index):
        return ref.at[pl.ds(pl.multiple_of(index * 16, 16), 16)]

    mine16 = pl.ds(pl.multiple_of(s * 16, 16), 16)
    load_frames.wait()
    for copy in small:
        copy.wait()
    for j in range(8):
        fs[pl.ds(j, T, stride=8), :] = frames[:, j * 128:(j + 1) * 128].astype(jnp.float32)
    a2a_src[...] = fs[...].astype(jnp.bfloat16)
    a2a_dst[mine16, :] = a2a_src[mine16, :]
    ids_rows = jnp.concatenate([ids_in[...].astype(jnp.float32), jnp.zeros((HD - 3, T), jnp.float32)], axis=0).T
    for k in range(NS):
        ids_src[k] = ids_rows[2 * k:2 * k + 2, :]
    ids_buf[pl.ds(s, 1)] = ids_src[pl.ds(s, 1)]
    for row, ref in enumerate((bq, bk, bv)):
        biases[row:row + 1, :] = ref[...].astype(jnp.float32).reshape(1, 512)
    load_qa.wait()
    load_qb.wait()
    load_k.wait()
    pl.semaphore_wait(barrier, NS - 1 + NM - 1)

    def a2a_copy(dst_dev, src_block, dst_block):
        return pltpu.make_async_remote_copy(
            src_ref=block16(a2a_src, src_block), dst_ref=block16(a2a_dst, dst_block),
            send_sem=sa_s.at[0], recv_sem=sa_r.at[0], device_id=(dst_dev, m), device_id_type=MESH,
        )

    @pl.loop(1, NS)
    def _(k):
        a2a_copy(lax.rem(s + k, NS), lax.rem(s + k, NS), s).start()

    a2a_all = pltpu.make_async_remote_copy(
        src_ref=a2a_src.at[pl.ds(0, (NS - 1) * 16)], dst_ref=a2a_dst.at[pl.ds(0, (NS - 1) * 16)],
        send_sem=sa_s.at[0], recv_sem=sa_r.at[0], device_id=((s + 1) % NS, m), device_id_type=MESH,
    )

    def id_copy(target, k):
        return pltpu.make_async_remote_copy(
            src_ref=ids_src.at[target], dst_ref=ids_buf.at[s],
            send_sem=si_s.at[k], recv_sem=si_r.at[0], device_id=(target, m), device_id_type=MESH,
        )

    @pl.loop(0, NZ)
    def _(k):
        target = k * 8 + m

        @pl.when(target != s)
        def _():
            id_copy(target, k).start()

    wg.start_b()
    wg.start_a()
    drain(wg.b_arrive(1))
    drain(wg.first())
    a2a_all.wait_recv()
    fs[...] = a2a_dst[...].astype(jnp.float32)
    for j in range(8):
        tok[m, :, j * 128:(j + 1) * 128] = fs[pl.ds(j, T, stride=8), :].astype(jnp.bfloat16)

    def y_send(d, half, way):
        part = tok.at[(m + d + NM) % NM, pl.ds(half * 64, 64)]
        pltpu.make_async_remote_copy(
            src_ref=part, dst_ref=part, send_sem=sy_s.at[0],
            recv_sem=sy_r.at[(d - way) % NM, half], device_id=(s, (m + way + NM) % NM), device_id_type=MESH,
        ).start()

    def y_wait(d, half):
        part = tok.at[(m + d + NM) % NM, pl.ds(half * 64, 64)]
        pltpu.make_async_remote_copy(
            src_ref=part, dst_ref=part, send_sem=sy_s.at[0], recv_sem=sy_r.at[d % NM, half],
            device_id=(s, (m + 1) % NM), device_id_type=MESH,
        ).wait_recv()

    line_a[...] = jnp.zeros_like(line_a)
    line_b[...] = jnp.zeros_like(line_b)
    acc[...] = jnp.zeros_like(acc)
    den[...] = jnp.zeros_like(den)
    mx[...] = jnp.full(mx.shape, -1e30, jnp.float32)
    squares = jnp.zeros((T, HD), jnp.float32)
    for j in range(8):
        part = tok[m, :, j * 128:(j + 1) * 128].astype(jnp.float32)
        squares = squares + part * part
    sums_src[...] = jnp.broadcast_to(jnp.sum(squares.T, axis=0, keepdims=True), (8, T))
    sums[pl.ds(m, 1)] = sums_src[...][None]

    def sums_copy(way_k):
        return pltpu.make_async_remote_copy(
            src_ref=sums_src, dst_ref=sums.at[m], send_sem=sq_s.at[way_k], recv_sem=sq_r.at[0],
            device_id=(s, (m + way_k) % NM), device_id_type=MESH,
        )

    @pl.loop(1, NM)
    def _(k):
        sums_copy(k).start()

    for half in (0, 1):
        for way in (1, -1):
            y_send(0, half, way)

    def find_inverse():
        pltpu.make_async_remote_copy(
            src_ref=sums.at[pl.ds(0, NM - 1)], dst_ref=sums.at[pl.ds(0, NM - 1)], send_sem=sq_s.at[0],
            recv_sem=sq_r.at[0], device_id=(s, (m + 1) % NM), device_id_type=MESH,
        ).wait_recv()
        total = sums[0]
        for k in range(1, NM):
            total = total + sums[k]
        row = lax.rsqrt(total[0:1, :] / (NM * 1024.0) + 1e-06)
        inverse[...] = jnp.broadcast_to(row, (T, T)).T

    def normalise(d, half):
        b = (m + d + NM) % NM
        rows = pl.ds(half * 64, 64)
        scale = gain[pl.ds(pl.multiple_of(b * 1024, 1024), 1024)].astype(jnp.float32).reshape(1, 1024)
        column = inverse[rows, 0:1]
        nrm[b, rows, :] = (tok[b, rows, :].astype(jnp.float32) * column * scale).astype(jnp.bfloat16)

    def y_steps():
        find_inverse()
        for half in (0, 1):
            normalise(0, half)
        for k in (1, 2, 3, 4):
            for half in (0, 1):
                for d in DIST[k]:
                    y_wait(d, half)
                    way = -1 if d > 0 else 1
                    if k < 3 or (k == 3 and way == (1 if half == 0 else -1)):
                        y_send(d, half, way)
                    normalise(d, half)
                    yield

    def p_copy(way_k):
        return pltpu.make_async_remote_copy(
            src_ref=ids_t, dst_ref=ids_t, send_sem=sp_s.at[way_k],
            recv_sem=sp_r.at[0], device_id=(s, (m + way_k) % NM), device_id_type=MESH,
        )

    collector = s % NM == m

    def collect_ids():
        @pl.when(collector)
        def _():
            pltpu.make_async_remote_copy(
                src_ref=ids_src.at[pl.ds(0, NS - 1)], dst_ref=ids_buf.at[pl.ds(0, NS - 1)],
                send_sem=si_s.at[0], recv_sem=si_r.at[0], device_id=((s + 1) % NS, m), device_id_type=MESH,
            ).wait_recv()
            for src in range(NS):
                ids_dense[2 * src:2 * src + 2, :] = ids_buf[src]
            ids_t[...] = ids_dense[...].T[0:8, :]

            @pl.loop(1, NM)
            def _(k):
                p_copy(k).start()

    def make_tables():
        @pl.when(jnp.logical_not(collector))
        def _():
            p_copy(1).wait_recv()

        lane = lax.broadcasted_iota(jnp.int32, (T, HD), 1)
        front = lane < HD // 2
        place = jnp.where(front, lane, lane - HD // 2)
        columns = jnp.concatenate([ids_t[...], jnp.zeros((HD - 8, T), jnp.float32)], axis=0).T
        chosen = jnp.where(place < 16, columns[:, 0:1], jnp.where(place < 40, columns[:, 1:2], columns[:, 2:3]))
        angle = chosen * freq[...]
        sines = jnp.sin(angle)
        tables[0] = jnp.cos(angle)
        tables[1] = jnp.where(front, -sines, sines)

    def weight_steps():
        yield from wg.b_arrive(2)
        yield from wg.b_across(0)
        yield from wg.a_arrive(1)
        collect_ids()
        yield from wg.b_across(1)
        yield from wg.b_last(0)
        yield from wg.b_arrive(3)
        yield from wg.b_arrive(4)
        yield from wg.b_across(2)
        yield from wg.b_last(1)
        yield from wg.a_arrive(2)
        yield from wg.b_across(3)
        yield from wg.b_last(2)
        yield from wg.a_arrive(3)
        make_tables()
    def of_core(block, core):
        cols = [block[:, (k * 2 + core) * T:(k * 2 + core + 1) * T] for k in range(NX)]
        return jnp.concatenate(cols, axis=1)

    def project(dz):
        b = wg.at_z(dz)
        wg.wait_sib(0, dz)
        wg.wait_sib(1, dz)
        normed = nrm[b]
        for core in (0, 1):
            rows = pl.ds(pl.multiple_of((core * NZ + b) * NX * T, NX * T), NX * T)
            part = of_core(normed, core)
            line_b[...] += jnp.dot(part, wb[rows, :], preferred_element_type=jnp.float32)
            line_a[...] += jnp.dot(part, wa[rows, :], preferred_element_type=jnp.float32)

    ring = y_steps()
    for index, _ in enumerate(weight_steps()):
        if index % 3 == 2:
            next(ring, None)
    drain(ring)
    drain(wg.b_across(4))
    project(0)
    drain(wg.b_last(3))
    project(-1)
    project(1)
    drain(wg.a_arrive(4))
    drain(wg.b_last(4))
    for dz in (-2, 2, -3, 3, 4):
        project(dz)

    def rotate(part):
        return part * tables[0] + pltpu.roll(part, HD // 2, axis=1) * tables[1]

    linear = line_b[:, 512 - CA:CB] + jnp.where(is_key, biases[1:2, head_cols], biases[2:3, head_cols])
    own_kind[own, :] = jnp.where(is_key, rotate(linear), linear).astype(jnp.bfloat16)

    exchange = pltpu.make_async_remote_copy(
        src_ref=own_kind.at[own], dst_ref=other_kind.at[own], send_sem=se.at[0], recv_sem=se.at[1],
        device_id=(s, m + 1 - 2 * (m % 2)), device_id_type=MESH,
    )
    exchange.start()
    kg.start_b()


    for h in range(4):
        part = (line_a, line_b)[h // 2][:, (h % 2) * HD:(h % 2 + 1) * HD]
        qs[h] = rotate(part + biases[0:1, h * HD:(h + 1) * HD]).astype(jnp.bfloat16)

    exchange.wait_recv()
    kg.start_a()
    key_base = jnp.where(is_key, 0, NS * T)

    def slab_body(zz, masked):
        def rows_of(base, core):
            return pl.ds(pl.multiple_of(base + (core * NZ + zz) * NX * T, NX * T), NX * T)

        @pl.loop(0, 4)
        def _(h):
            scores = jnp.concatenate(
                [
                    lax.dot_general(
                        qs[h], kv[rows_of(key_base, core), :], (((1,), (1,)), ((), ())),
                        preferred_element_type=jnp.float32,
                    )
                    for core in (0, 1)
                ],
                axis=1,
            )
            if masked:
                row = lax.broadcasted_iota(jnp.int32, scores.shape, 0) + (x * 2 + c) * T
                lane = lax.broadcasted_iota(jnp.int32, scores.shape, 1)
                blk = lane // T
                key = jnp.where(blk < NX, blk * 2, (blk - NX) * 2 + 1) * T + (lane - blk * T)
                visible = key <= row
                scores = jnp.where(visible, scores, -1e30)
            old = mx[h][:, 0:1]
            new = jnp.maximum(old, jnp.max(scores, axis=1, keepdims=True))
            factor = jnp.exp2((old - new) * EXP_SCALE)
            terms = jnp.exp2((scores - new) * EXP_SCALE)
            if masked:
                terms = jnp.where(visible, terms, 0.0)
            total = den[h][:, 0:1] * factor + jnp.sum(terms, axis=1, keepdims=True)
            probs = terms.astype(jnp.bfloat16)
            mixed = acc[h] * factor
            for core in (0, 1):
                mixed = mixed + jnp.dot(
                    probs[:, core * NX * T:(core + 1) * NX * T], kv[rows_of(NS * T - key_base, core), :],
                    preferred_element_type=jnp.float32,
                )
            acc[h] = mixed
            mx[h] = jnp.broadcast_to(new, (T, HD))
            den[h] = jnp.broadcast_to(total, (T, HD))

    def slab(k):
        for dz in DIST[k]:
            kg.wait_sib(0, dz)
            kg.wait_sib(1, dz)
            if dz == 0:
                slab_body(z, True)
            else:
                zz = (z + dz + NZ) % NZ

                @pl.when(zz < z)
                def _():
                    slab_body(zz, False)

    drain(kg.b_arrive(1))
    drain(kg.first())
    drain(kg.b_arrive(2))
    drain(kg.b_across(0))
    drain(kg.b_last(0))
    drain(kg.b_arrive(3))
    drain(kg.a_arrive(1))
    drain(kg.b_arrive(4))
    drain(kg.b_across(1))
    drain(kg.b_last(1))
    slab(0)
    drain(kg.a_arrive(2))
    drain(kg.b_across(2))
    drain(kg.b_last(2))
    slab(1)
    drain(kg.a_arrive(3))
    drain(kg.b_across(3))
    drain(kg.b_last(3))
    slab(2)
    drain(kg.a_arrive(4))
    drain(kg.b_across(4))
    drain(kg.b_last(4))
    slab(3)
    slab(4)

    for h in range(4):
        out[:, h * HD:(h + 1) * HD] = (acc[h] / den[h]).astype(jnp.bfloat16)

    a2a_all.wait_send()

    @pl.loop(0, NZ)
    def _(k):
        target = k * 8 + m

        @pl.when(target != s)
        def _():
            id_copy(target, k).wait_send()

    @pl.when(collector)
    def _():
        @pl.loop(1, NM)
        def _(k):
            p_copy(k).wait_send()

    @pl.loop(1, NM)
    def _(k):
        sums_copy(k).wait_send()

    exchange.wait_send()
    seven = tok.at[pl.ds(0, 7)]
    pltpu.make_async_remote_copy(
        src_ref=seven, dst_ref=seven, send_sem=sy_s.at[0], recv_sem=sy_r.at[0, 0],
        device_id=(s, (m + 1) % NM), device_id_type=MESH,
    ).wait_send()
    wg.finish()
    kg.finish()


def gather_sems():
    dma = pltpu.SemaphoreType.DMA
    return [dma((NZ, NX)), dma((NZ, NX)), dma((NZ,)), dma((NZ,)), dma((2,)), dma((2,))]


def shards(frames_tokens, positions, norm_gain, w_query, w_key, w_value, b_query, b_key, b_value):
    dma = pltpu.SemaphoreType.DMA
    half = np.power(1000000.0, -(2.0 * np.arange(HD // 2)) / HD).astype(np.float32)
    freq = jnp.asarray(np.concatenate([half, half])[None, :])
    vmem = pl.BlockSpec(memory_space=pltpu.VMEM)
    hbm = pl.BlockSpec(memory_space=pltpu.HBM)
    return pl.pallas_call(
        kernel,
        name="fused",
        out_shape=jax.ShapeDtypeStruct((T, 512), jnp.bfloat16),
        in_specs=[hbm] * 10,
        out_specs=vmem,
        scratch_shapes=[
            pltpu.VMEM((T, 1024), jnp.bfloat16),
            pltpu.VMEM((3, T), jnp.int32),
            pltpu.VMEM((NS * T,), jnp.bfloat16),
            pltpu.VMEM((512,), jnp.bfloat16),
            pltpu.VMEM((512,), jnp.bfloat16),
            pltpu.VMEM((512,), jnp.bfloat16),
            pltpu.VMEM((1, HD), jnp.float32),
            pltpu.VMEM((1024, 128), jnp.float32),
            pltpu.VMEM((1024, 128), jnp.bfloat16),
            pltpu.VMEM((1024, 128), jnp.bfloat16),
            pltpu.VMEM((NS, 2, HD), jnp.float32),
            pltpu.VMEM((NS, 2, HD), jnp.float32),
            pltpu.VMEM((T, HD), jnp.float32),
            pltpu.VMEM((8, T), jnp.float32),
            pltpu.VMEM((NM, T, 1024), jnp.bfloat16),
            pltpu.VMEM((NM, T, 1024), jnp.bfloat16),
            pltpu.VMEM((NS * T, CA), jnp.bfloat16),
            pltpu.VMEM((NS * T, CB), jnp.bfloat16),
            pltpu.VMEM((2 * NS * T, HD), jnp.bfloat16),
            pltpu.VMEM((4, T, HD), jnp.bfloat16),
            pltpu.VMEM((4, T, HD), jnp.float32),
            pltpu.VMEM((4, T, HD), jnp.float32),
            pltpu.VMEM((4, T, HD), jnp.float32),
            pltpu.VMEM((T, CA), jnp.float32),
            pltpu.VMEM((T, CB), jnp.float32),
            pltpu.VMEM((T, T), jnp.float32),
            pltpu.VMEM((8, T), jnp.float32),
            pltpu.VMEM((NM, 8, T), jnp.float32),
            pltpu.VMEM((2, T, HD), jnp.float32),
            pltpu.VMEM((8, 512), jnp.float32),
            dma((10,)), dma((NM,)), dma((1,)), dma((1,)), dma((1,)), dma((NZ,)), dma((1,)),
            dma((1,)), dma((NM, 2)), dma((NM,)), dma((1,)), dma((2,)),
        ] + gather_sems() + gather_sems(),
        compiler_params=pltpu.CompilerParams(
            collective_id=0, has_side_effects=True, vmem_limit_bytes=64 * 2**20 - 2**17
        ),
        cost_estimate=pl.CostEstimate(flops=5 * 10**9, bytes_accessed=10**7, transcendentals=4 * 10**6),
    )(
        frames_tokens, positions.T, norm_gain, w_query, w_key, w_value, b_query, b_key, b_value, freq,
    )


def solution(mesh):
    in_specs = (
        P("seq", "mp"), P("seq", None), P(), P("seq", "mp"), P("seq", None), P("seq", None),
        P("mp"), P(), P(),
    )
    return jax.shard_map(shards, mesh=mesh, in_specs=in_specs, out_specs=P("seq", "mp"), check_vma=False)
```

```python
import functools
import math

import jax
import jax.numpy as jnp
import numpy as np
from jax import lax
from jax.experimental import pallas as pl
from jax.experimental.pallas import tpu as pltpu
from jax.sharding import PartitionSpec as P

HD = 128
T = 128
NX, NZ, NM = 4, 8, 8
NS = NZ * NX * 2
CA, CB = 256, 384
MESH = pl.DeviceIdType.MESH
DIST = [[0], [-1, 1], [-2, 2], [-3, 3], [4]]
EXP_SCALE = math.log2(math.e) / math.sqrt(HD)


class Gather:
    def __init__(self, a, b, sems, z, x, c, m, direct_b):
        self.a, self.b = a, b
        self.ra, self.rb, self.ca, self.cb, self.sa, self.sb = sems
        self.z, self.x, self.c, self.m = z, x, c, m
        self.dir = 1 - 2 * c
        self.direct_b = direct_b
        self.zs = [lax.rem(z + dz, NZ) for dz in range(NZ)]
        self.xs = [lax.rem(x + dx, NX) for dx in range(NX)]

    def rows(self, ref, dz, dx, core):
        block = (core * NZ + self.at_z(dz)) * NX + self.xs[dx % NX]
        return ref.at[pl.ds(pl.multiple_of(block * T, T), T)]

    def four(self, ref, dz, core):
        first = (core * NZ + self.at_z(dz)) * NX
        return ref.at[pl.ds(pl.multiple_of(first * T, NX * T), NX * T)]

    def dev(self, dz, dx, core):
        return ((self.at_z(dz) * NX + self.xs[dx % NX]) * 2 + core, self.m)

    def at_z(self, dz):
        return self.zs[dz % NZ] if isinstance(dz, int) else lax.rem(self.z + dz + NZ, NZ)

    def copy(self, part, send_sem, recv_sem, device):
        return pltpu.make_async_remote_copy(
            src_ref=part, dst_ref=part, send_sem=send_sem, recv_sem=recv_sem,
            device_id=device, device_id_type=MESH,
        )

    def send(self, ref, dz, dx, to_z, to_x, recv, send_sem):
        self.copy(self.rows(ref, dz, dx, self.c), send_sem, recv, self.dev(to_z, to_x, self.c)).start()

    def a_z(self, dz, dx, way):
        self.send(self.a, dz, dx, way, 0, self.ra.at[(dz - way) % NZ, dx % NX], self.sa.at[0])

    def a_x(self, to_x):
        self.send(self.a, 0, 0, 0, to_x, self.ra.at[0, (-to_x) % NX], self.sa.at[0])

    def b_z(self, dz, way):
        self.send(self.b, dz, 0, way, 0, self.rb.at[(dz - way) % NZ, 0], self.sb.at[0])

    def b_z_far(self):
        self.send(self.b, -2 * self.dir, 0, 2 * self.dir, 0, self.rb.at[4, 0], self.sb.at[0])

    def straight(self, dz):
        return self.direct_b or dz == 4

    def b_x(self, dz):
        for to_x in (1, 3, 2) if self.straight(dz) else (1, 3):
            self.send(self.b, dz, 0, 0, to_x, self.rb.at[dz % NZ, (-to_x) % NX], self.sb.at[0])

    def sib(self, which, dz):
        ref, recv, send = (self.a, self.ca, self.sa) if which == 0 else (self.b, self.cb, self.sb)
        self.copy(self.four(ref, dz, self.c), send.at[1], recv.at[dz % NZ], self.dev(0, 0, 1 - self.c)).start()

    def wait(self, which, dz, dx):
        ref, recv, send = (self.a, self.ra, self.sa) if which == 0 else (self.b, self.rb, self.sb)
        self.copy(
            self.rows(ref, dz, dx, self.c), send.at[0], recv.at[dz % NZ, dx % NX], self.dev(0, 0, 1 - self.c)
        ).wait_recv()

    def wait_sib(self, which, dz):
        ref, recv, send = (self.a, self.ca, self.sa) if which == 0 else (self.b, self.cb, self.sb)
        self.copy(
            self.four(ref, dz, 1 - self.c), send.at[1], recv.at[dz % NZ], self.dev(0, 0, 1 - self.c)
        ).wait_recv()

    def start_a(self):
        for to_x in (1, 3, 2):
            self.a_x(to_x)
        for way in (1, -1):
            self.a_z(0, 0, way)

    def start_b(self):
        for way in (1, -1, 2, -2, 3, -3, 4) if self.direct_b else (1, -1, 2, -2):
            self.b_z(0, way)
        self.b_x(0)

    def first(self):
        for dx in (1, 3, 2):
            self.wait(0, 0, dx)
            for way in (1, -1):
                self.a_z(0, dx, way)
            yield
        self.sib(0, 0)

    def b_arrive(self, k):
        for dz in DIST[k]:
            self.wait(1, dz, 0)
            if k == 2 and not self.direct_b:
                self.b_z(dz, -1 if dz > 0 else 1)
            self.b_x(dz)
            yield
        if k == 2 and not self.direct_b:
            self.b_z_far()

    def b_across(self, k):
        for dz in DIST[k]:
            for dx in (1, 3):
                self.wait(1, dz, dx)
                if not self.straight(dz) and dx == (3 if dz % 2 == 0 else 1):
                    way = 1 if dx == 3 else -1
                    self.send(self.b, dz, dx, 0, way, self.rb.at[dz % NZ, 2], self.sb.at[0])
                yield

    def b_last(self, k):
        for dz in DIST[k]:
            self.wait(1, dz, 2)
            self.sib(1, dz)
            yield

    def a_arrive(self, k):
        for dx in (0, 1, 3, 2):
            for dz in DIST[k]:
                self.wait(0, dz, dx)
                way = -1 if dz > 0 else 1
                if k < 3 or (k == 3 and way == (1 if dx % 2 == 0 else -1)):
                    self.a_z(dz, dx, way)
                yield
        for dz in DIST[k]:
            self.sib(0, dz)

    def finish(self):
        for ref, send in ((self.a, self.sa), (self.b, self.sb)):
            for k, count in ((0, 31), (1, 32)):
                self.copy(ref.at[pl.ds(0, count * T)], send.at[k], send.at[k], self.dev(0, 0, 1 - self.c)).wait_send()


def drain(steps):
    for _ in steps:
        pass


def kernel(
    frames_in, ids_hbm, gain_hbm, wq, wk, wv, bq_hbm, bk_hbm, bv_hbm, freq_hbm, out,
    frames, ids_in, gain, bq, bk, bv, freq, fs, a2a_src, a2a_dst, ids_src, ids_buf, ids_dense, ids_t, tok, nrm, wa, wb, kv, qs, acc, mx, den,
    line_a, line_b, inverse, sums_src, sums, tables, biases, s_in, sq_s, sq_r, sa_s, sa_r, si_s, si_r, sy_s, sy_r, sp_s, sp_r, se,
    *gsems,
):
    s = lax.axis_index("seq")
    m = lax.axis_index("mp")
    z, x, c = s // (NX * 2), (s // 2) % NX, s % 2
    wg = Gather(wa, wb, gsems[:6], z, x, c, m, False)
    own_kind, other_kind = kv.at[pl.ds(0, NS * T)], kv.at[pl.ds(NS * T, NS * T)]
    kg = Gather(other_kind, own_kind, gsems[6:], z, x, c, m, True)

    barrier = pltpu.get_barrier_semaphore()

    block = (c * NZ + z) * NX + x
    own = pl.ds(pl.multiple_of(block * T, T), T)
    head_cols = pl.ds(pl.multiple_of((m // 2) * HD, HD), HD)
    is_key = m % 2 == 0
    load_frames = pltpu.make_async_copy(frames_in, frames, s_in.at[0])
    load_qa = pltpu.make_async_copy(wq.at[:, pl.ds(0, CA)], wa.at[own], s_in.at[1])
    load_qb = pltpu.make_async_copy(wq.at[:, pl.ds(CA, 512 - CA)], wb.at[own, pl.ds(0, 512 - CA)], s_in.at[2])
    load_k = pltpu.make_async_copy(wk.at[:, head_cols], wb.at[own, pl.ds(512 - CA, HD)], s_in.at[3])
    load_v = pltpu.make_async_copy(wv.at[:, head_cols], wb.at[own, pl.ds(512 - CA, HD)], s_in.at[3])
    small = [
        pltpu.make_async_copy(src, dst, s_in.at[4 + k])
        for k, (src, dst) in enumerate(
            ((ids_hbm, ids_in), (gain_hbm, gain), (bq_hbm, bq), (bk_hbm, bk), (bv_hbm, bv), (freq_hbm, freq))
        )
    ]
    load_frames.start()
    for copy in small:
        copy.start()
    load_qa.start()
    load_qb.start()

    @pl.when(is_key)
    def _():
        load_k.start()

    @pl.when(jnp.logical_not(is_key))
    def _():
        load_v.start()

    @pl.loop(1, NS)
    def _(k):
        pl.semaphore_signal(barrier, inc=1, device_id=(lax.rem(s + k, NS), m), device_id_type=MESH)

    @pl.loop(1, NM)
    def _(k):
        pl.semaphore_signal(barrier, inc=1, device_id=(s, lax.rem(m + k, NM)), device_id_type=MESH)

    def block16(ref, index):
        return ref.at[pl.ds(pl.multiple_of(index * 16, 16), 16)]

    mine16 = pl.ds(pl.multiple_of(s * 16, 16), 16)
    load_frames.wait()
    for copy in small:
        copy.wait()
    for j in range(8):
        fs[pl.ds(j, T, stride=8), :] = frames[:, j * 128:(j + 1) * 128].astype(jnp.float32)
    a2a_src[...] = fs[...].astype(jnp.bfloat16)
    a2a_dst[mine16, :] = a2a_src[mine16, :]
    ids_rows = jnp.concatenate([ids_in[...].astype(jnp.float32), jnp.zeros((HD - 3, T), jnp.float32)], axis=0).T
    for k in range(NS):
        ids_src[k] = ids_rows[2 * k:2 * k + 2, :]
    ids_buf[pl.ds(s, 1)] = ids_src[pl.ds(s, 1)]
    for row, ref in enumerate((bq, bk, bv)):
        biases[row:row + 1, :] = ref[...].astype(jnp.float32).reshape(1, 512)
    load_qa.wait()
    load_qb.wait()
    load_k.wait()
    pl.semaphore_wait(barrier, NS - 1 + NM - 1)

    def a2a_copy(dst_dev, src_block, dst_block):
        return pltpu.make_async_remote_copy(
            src_ref=block16(a2a_src, src_block), dst_ref=block16(a2a_dst, dst_block),
            send_sem=sa_s.at[0], recv_sem=sa_r.at[0], device_id=(dst_dev, m), device_id_type=MESH,
        )

    @pl.loop(1, NS)
    def _(k):
        a2a_copy(lax.rem(s + k, NS), lax.rem(s + k, NS), s).start()

    a2a_all = pltpu.make_async_remote_copy(
        src_ref=a2a_src.at[pl.ds(0, (NS - 1) * 16)], dst_ref=a2a_dst.at[pl.ds(0, (NS - 1) * 16)],
        send_sem=sa_s.at[0], recv_sem=sa_r.at[0], device_id=((s + 1) % NS, m), device_id_type=MESH,
    )

    def id_copy(target, k):
        return pltpu.make_async_remote_copy(
            src_ref=ids_src.at[target], dst_ref=ids_buf.at[s],
            send_sem=si_s.at[k], recv_sem=si_r.at[0], device_id=(target, m), device_id_type=MESH,
        )

    @pl.loop(0, NZ)
    def _(k):
        target = k * 8 + m

        @pl.when(target != s)
        def _():
            id_copy(target, k).start()

    wg.start_b()
    wg.start_a()
    drain(wg.b_arrive(1))
    drain(wg.first())
    a2a_all.wait_recv()
    fs[...] = a2a_dst[...].astype(jnp.float32)
    for j in range(8):
        tok[m, :, j * 128:(j + 1) * 128] = fs[pl.ds(j, T, stride=8), :].astype(jnp.bfloat16)

    def y_send(d, half, way):
        part = tok.at[(m + d + NM) % NM, pl.ds(half * 64, 64)]
        pltpu.make_async_remote_copy(
            src_ref=part, dst_ref=part, send_sem=sy_s.at[0],
            recv_sem=sy_r.at[(d - way) % NM, half], device_id=(s, (m + way + NM) % NM), device_id_type=MESH,
        ).start()

    def y_wait(d, half):
        part = tok.at[(m + d + NM) % NM, pl.ds(half * 64, 64)]
        pltpu.make_async_remote_copy(
            src_ref=part, dst_ref=part, send_sem=sy_s.at[0], recv_sem=sy_r.at[d % NM, half],
            device_id=(s, (m + 1) % NM), device_id_type=MESH,
        ).wait_recv()

    line_a[...] = jnp.zeros_like(line_a)
    line_b[...] = jnp.zeros_like(line_b)
    acc[...] = jnp.zeros_like(acc)
    den[...] = jnp.zeros_like(den)
    mx[...] = jnp.full(mx.shape, -1e30, jnp.float32)
    squares = jnp.zeros((T, HD), jnp.float32)
    for j in range(8):
        part = tok[m, :, j * 128:(j + 1) * 128].astype(jnp.float32)
        squares = squares + part * part
    sums_src[...] = jnp.broadcast_to(jnp.sum(squares.T, axis=0, keepdims=True), (8, T))
    sums[pl.ds(m, 1)] = sums_src[...][None]

    def sums_copy(way_k):
        return pltpu.make_async_remote_copy(
            src_ref=sums_src, dst_ref=sums.at[m], send_sem=sq_s.at[way_k], recv_sem=sq_r.at[0],
            device_id=(s, (m + way_k) % NM), device_id_type=MESH,
        )

    @pl.loop(1, NM)
    def _(k):
        sums_copy(k).start()

    for half in (0, 1):
        for way in (1, -1):
            y_send(0, half, way)

    def find_inverse():
        pltpu.make_async_remote_copy(
            src_ref=sums.at[pl.ds(0, NM - 1)], dst_ref=sums.at[pl.ds(0, NM - 1)], send_sem=sq_s.at[0],
            recv_sem=sq_r.at[0], device_id=(s, (m + 1) % NM), device_id_type=MESH,
        ).wait_recv()
        total = sums[0]
        for k in range(1, NM):
            total = total + sums[k]
        row = lax.rsqrt(total[0:1, :] / (NM * 1024.0) + 1e-06)
        inverse[...] = jnp.broadcast_to(row, (T, T)).T

    def normalise(d, half):
        b = (m + d + NM) % NM
        rows = pl.ds(half * 64, 64)
        scale = gain[pl.ds(pl.multiple_of(b * 1024, 1024), 1024)].astype(jnp.float32).reshape(1, 1024)
        column = inverse[rows, 0:1]
        nrm[b, rows, :] = (tok[b, rows, :].astype(jnp.float32) * column * scale).astype(jnp.bfloat16)

    def y_steps():
        find_inverse()
        for half in (0, 1):
            normalise(0, half)
        for k in (1, 2, 3, 4):
            for half in (0, 1):
                for d in DIST[k]:
                    y_wait(d, half)
                    way = -1 if d > 0 else 1
                    if k < 3 or (k == 3 and way == (1 if half == 0 else -1)):
                        y_send(d, half, way)
                    normalise(d, half)
                    yield

    def p_copy(way_k):
        return pltpu.make_async_remote_copy(
            src_ref=ids_t, dst_ref=ids_t, send_sem=sp_s.at[way_k],
            recv_sem=sp_r.at[0], device_id=(s, (m + way_k) % NM), device_id_type=MESH,
        )

    collector = s % NM == m

    def collect_ids():
        @pl.when(collector)
        def _():
            pltpu.make_async_remote_copy(
                src_ref=ids_src.at[pl.ds(0, NS - 1)], dst_ref=ids_buf.at[pl.ds(0, NS - 1)],
                send_sem=si_s.at[0], recv_sem=si_r.at[0], device_id=((s + 1) % NS, m), device_id_type=MESH,
            ).wait_recv()
            for src in range(NS):
                ids_dense[2 * src:2 * src + 2, :] = ids_buf[src]
            ids_t[...] = ids_dense[...].T[0:8, :]

            @pl.loop(1, NM)
            def _(k):
                p_copy(k).start()

    def make_tables():
        @pl.when(jnp.logical_not(collector))
        def _():
            p_copy(1).wait_recv()

        lane = lax.broadcasted_iota(jnp.int32, (T, HD), 1)
        front = lane < HD // 2
        place = jnp.where(front, lane, lane - HD // 2)
        columns = jnp.concatenate([ids_t[...], jnp.zeros((HD - 8, T), jnp.float32)], axis=0).T
        chosen = jnp.where(place < 16, columns[:, 0:1], jnp.where(place < 40, columns[:, 1:2], columns[:, 2:3]))
        angle = chosen * freq[...]
        sines = jnp.sin(angle)
        tables[0] = jnp.cos(angle)
        tables[1] = jnp.where(front, -sines, sines)

    def weight_steps():
        yield from wg.b_arrive(2)
        yield from wg.b_across(0)
        yield from wg.a_arrive(1)
        collect_ids()
        yield from wg.b_across(1)
        yield from wg.b_last(0)
        yield from wg.b_arrive(3)
        yield from wg.b_arrive(4)
        yield from wg.b_across(2)
        yield from wg.b_last(1)
        yield from wg.a_arrive(2)
        yield from wg.b_across(3)
        yield from wg.b_last(2)
        yield from wg.a_arrive(3)
        make_tables()
    def of_core(block, core):
        cols = [block[:, (k * 2 + core) * T:(k * 2 + core + 1) * T] for k in range(NX)]
        return jnp.concatenate(cols, axis=1)

    def project(dz):
        b = wg.at_z(dz)
        wg.wait_sib(0, dz)
        wg.wait_sib(1, dz)
        normed = nrm[b]
        for core in (0, 1):
            rows = pl.ds(pl.multiple_of((core * NZ + b) * NX * T, NX * T), NX * T)
            part = of_core(normed, core)
            line_b[...] += jnp.dot(part, wb[rows, :], preferred_element_type=jnp.float32)
            line_a[...] += jnp.dot(part, wa[rows, :], preferred_element_type=jnp.float32)

    ring = y_steps()
    for index, _ in enumerate(weight_steps()):
        if index % 3 == 2:
            next(ring, None)
    drain(ring)
    drain(wg.b_across(4))
    project(0)
    drain(wg.b_last(3))
    project(-1)
    project(1)
    drain(wg.a_arrive(4))
    drain(wg.b_last(4))
    for dz in (-2, 2, -3, 3, 4):
        project(dz)

    def rotate(part):
        return part * tables[0] + pltpu.roll(part, HD // 2, axis=1) * tables[1]

    linear = line_b[:, 512 - CA:CB] + jnp.where(is_key, biases[1:2, head_cols], biases[2:3, head_cols])
    own_kind[own, :] = jnp.where(is_key, rotate(linear), linear).astype(jnp.bfloat16)

    exchange = pltpu.make_async_remote_copy(
        src_ref=own_kind.at[own], dst_ref=other_kind.at[own], send_sem=se.at[0], recv_sem=se.at[1],
        device_id=(s, m + 1 - 2 * (m % 2)), device_id_type=MESH,
    )
    exchange.start()
    kg.start_b()


    for h in range(4):
        part = (line_a, line_b)[h // 2][:, (h % 2) * HD:(h % 2 + 1) * HD]
        qs[h] = rotate(part + biases[0:1, h * HD:(h + 1) * HD]).astype(jnp.bfloat16)

    exchange.wait_recv()
    kg.start_a()
    key_base = jnp.where(is_key, 0, NS * T)

    def slab_body(zz, masked):
        def rows_of(base, core):
            return pl.ds(pl.multiple_of(base + (core * NZ + zz) * NX * T, NX * T), NX * T)

        for h in range(4):
            scores = jnp.concatenate(
                [
                    lax.dot_general(
                        qs[h], kv[rows_of(key_base, core), :], (((1,), (1,)), ((), ())),
                        preferred_element_type=jnp.float32,
                    )
                    for core in (0, 1)
                ],
                axis=1,
            )
            if masked:
                row = lax.broadcasted_iota(jnp.int32, scores.shape, 0) + (x * 2 + c) * T
                lane = lax.broadcasted_iota(jnp.int32, scores.shape, 1)
                blk = lane // T
                key = jnp.where(blk < NX, blk * 2, (blk - NX) * 2 + 1) * T + (lane - blk * T)
                visible = key <= row
                scores = jnp.where(visible, scores, -1e30)
            old = mx[h][:, 0:1]
            new = jnp.maximum(old, jnp.max(scores, axis=1, keepdims=True))
            factor = jnp.exp2((old - new) * EXP_SCALE)
            terms = jnp.exp2((scores - new) * EXP_SCALE)
            if masked:
                terms = jnp.where(visible, terms, 0.0)
            total = den[h][:, 0:1] * factor + jnp.sum(terms, axis=1, keepdims=True)
            probs = terms.astype(jnp.bfloat16)
            mixed = acc[h] * factor
            for core in (0, 1):
                mixed = mixed + jnp.dot(
                    probs[:, core * NX * T:(core + 1) * NX * T], kv[rows_of(NS * T - key_base, core), :],
                    preferred_element_type=jnp.float32,
                )
            acc[h] = mixed
            mx[h] = jnp.broadcast_to(new, (T, HD))
            den[h] = jnp.broadcast_to(total, (T, HD))

    def slab(k):
        for dz in DIST[k]:
            kg.wait_sib(0, dz)
            kg.wait_sib(1, dz)
            if dz == 0:
                slab_body(z, True)
            else:
                zz = (z + dz + NZ) % NZ

                @pl.when(zz < z)
                def _():
                    slab_body(zz, False)

    drain(kg.b_arrive(1))
    drain(kg.first())
    drain(kg.b_arrive(2))
    drain(kg.b_across(0))
    drain(kg.b_last(0))
    drain(kg.b_arrive(3))
    drain(kg.a_arrive(1))
    drain(kg.b_arrive(4))
    drain(kg.b_across(1))
    drain(kg.b_last(1))
    slab(0)
    drain(kg.a_arrive(2))
    drain(kg.b_across(2))
    drain(kg.b_last(2))
    slab(1)
    drain(kg.a_arrive(3))
    drain(kg.b_across(3))
    drain(kg.b_last(3))
    slab(2)
    drain(kg.a_arrive(4))
    drain(kg.b_across(4))
    drain(kg.b_last(4))
    slab(3)
    slab(4)

    for h in range(4):
        out[:, h * HD:(h + 1) * HD] = (acc[h] / den[h]).astype(jnp.bfloat16)

    a2a_all.wait_send()

    @pl.loop(0, NZ)
    def _(k):
        target = k * 8 + m

        @pl.when(target != s)
        def _():
            id_copy(target, k).wait_send()

    @pl.when(collector)
    def _():
        @pl.loop(1, NM)
        def _(k):
            p_copy(k).wait_send()

    @pl.loop(1, NM)
    def _(k):
        sums_copy(k).wait_send()

    exchange.wait_send()
    seven = tok.at[pl.ds(0, 7)]
    pltpu.make_async_remote_copy(
        src_ref=seven, dst_ref=seven, send_sem=sy_s.at[0], recv_sem=sy_r.at[0, 0],
        device_id=(s, (m + 1) % NM), device_id_type=MESH,
    ).wait_send()
    wg.finish()
    kg.finish()


def gather_sems():
    dma = pltpu.SemaphoreType.DMA
    return [dma((NZ, NX)), dma((NZ, NX)), dma((NZ,)), dma((NZ,)), dma((2,)), dma((2,))]


def shards(frames_tokens, positions, norm_gain, w_query, w_key, w_value, b_query, b_key, b_value):
    dma = pltpu.SemaphoreType.DMA
    half = np.power(1000000.0, -(2.0 * np.arange(HD // 2)) / HD).astype(np.float32)
    freq = jnp.asarray(np.concatenate([half, half])[None, :])
    vmem = pl.BlockSpec(memory_space=pltpu.VMEM)
    hbm = pl.BlockSpec(memory_space=pltpu.HBM)
    return pl.pallas_call(
        kernel,
        name="fused",
        out_shape=jax.ShapeDtypeStruct((T, 512), jnp.bfloat16),
        in_specs=[hbm] * 10,
        out_specs=vmem,
        scratch_shapes=[
            pltpu.VMEM((T, 1024), jnp.bfloat16),
            pltpu.VMEM((3, T), jnp.int32),
            pltpu.VMEM((NS * T,), jnp.bfloat16),
            pltpu.VMEM((512,), jnp.bfloat16),
            pltpu.VMEM((512,), jnp.bfloat16),
            pltpu.VMEM((512,), jnp.bfloat16),
            pltpu.VMEM((1, HD), jnp.float32),
            pltpu.VMEM((1024, 128), jnp.float32),
            pltpu.VMEM((1024, 128), jnp.bfloat16),
            pltpu.VMEM((1024, 128), jnp.bfloat16),
            pltpu.VMEM((NS, 2, HD), jnp.float32),
            pltpu.VMEM((NS, 2, HD), jnp.float32),
            pltpu.VMEM((T, HD), jnp.float32),
            pltpu.VMEM((8, T), jnp.float32),
            pltpu.VMEM((NM, T, 1024), jnp.bfloat16),
            pltpu.VMEM((NM, T, 1024), jnp.bfloat16),
            pltpu.VMEM((NS * T, CA), jnp.bfloat16),
            pltpu.VMEM((NS * T, CB), jnp.bfloat16),
            pltpu.VMEM((2 * NS * T, HD), jnp.bfloat16),
            pltpu.VMEM((4, T, HD), jnp.bfloat16),
            pltpu.VMEM((4, T, HD), jnp.float32),
            pltpu.VMEM((4, T, HD), jnp.float32),
            pltpu.VMEM((4, T, HD), jnp.float32),
            pltpu.VMEM((T, CA), jnp.float32),
            pltpu.VMEM((T, CB), jnp.float32),
            pltpu.VMEM((T, T), jnp.float32),
            pltpu.VMEM((8, T), jnp.float32),
            pltpu.VMEM((NM, 8, T), jnp.float32),
            pltpu.VMEM((2, T, HD), jnp.float32),
            pltpu.VMEM((8, 512), jnp.float32),
            dma((10,)), dma((NM,)), dma((1,)), dma((1,)), dma((1,)), dma((NZ,)), dma((1,)),
            dma((1,)), dma((NM, 2)), dma((NM,)), dma((1,)), dma((2,)),
        ] + gather_sems() + gather_sems(),
        compiler_params=pltpu.CompilerParams(
            collective_id=0, has_side_effects=True, vmem_limit_bytes=64 * 2**20 - 2**17
        ),
        cost_estimate=pl.CostEstimate(flops=5 * 10**9, bytes_accessed=10**7, transcendentals=4 * 10**6),
    )(
        frames_tokens, positions.T, norm_gain, w_query, w_key, w_value, b_query, b_key, b_value, freq,
    )


def solution(mesh):
    in_specs = (
        P("seq", "mp"), P("seq", None), P(), P("seq", "mp"), P("seq", None), P("seq", None),
        P("mp"), P(), P(),
    )
    return jax.shard_map(shards, mesh=mesh, in_specs=in_specs, out_specs=P("seq", "mp"), check_vma=False)
```
